256 devices in a mesh: dp: 128 (over x, y_hi, z, core), pair: 2 (over y_lo).
Axes of the slice: x: 4, y: 4 (y_hi: 2, y_lo: 2; y = y_hi * 2 + y_lo), z: 8, core: 2. Of those that a mesh axis runs over, the one named last changes fastest.
Arguments:
- tokens: bfloat16 [24576, 1792], P('dp'), may hold values from -6 to 6
- grad_out: bfloat16 [24576, 1792], P('dp'), may hold values from -6 to 6
- gate_probs: bfloat16 [24576, 2], P('dp'), may hold values from 0.049804688 to 1
- expert_ids: int32 [24576, 2], P('dp'), may hold values from 0 to 64, as said below
- route_slots: int32 [24576, 2], P('dp'), may hold values from 0 to 191, as said below
- hot_flags: int32 [65], replicated, may hold values from 0 to 1, as said below
- owner_slot: int32 [65], replicated, may hold values from 0 to 63, as said below
- cold_gate: bfloat16 [128, 640, 1792], P('dp', 'pair'), may hold values from -0.125 to 0.125
- cold_up: bfloat16 [128, 640, 1792], P('dp', 'pair'), may hold values from -0.125 to 0.125
- cold_down: bfloat16 [128, 640, 1792], P('dp', 'pair'), may hold values from -0.15625 to 0.15625
- hot_gate: bfloat16 [1280, 1792], P(('dp', 'pair')), may hold values from -0.125 to 0.125
- hot_up: bfloat16 [1280, 1792], P(('dp', 'pair')), may hold values from -0.125 to 0.125
- hot_down: bfloat16 [1280, 1792], P(('dp', 'pair')), may hold values from -0.15625 to 0.15625
Outputs:
- grad_tokens: bfloat16 [24576, 1792], P(('dp', 'pair'))
- grad_probs: float32 [24576, 2], P(('dp', 'pair'))
- grad_cold_gate: bfloat16 [128, 640, 1792], P('dp', 'pair')
- grad_cold_up: bfloat16 [128, 640, 1792], P('dp', 'pair')
- grad_cold_down: bfloat16 [128, 640, 1792], P('dp', 'pair')
- grad_hot_gate: bfloat16 [1280, 1792], P(('dp', 'pair'))
- grad_hot_up: bfloat16 [1280, 1792], P(('dp', 'pair'))
- grad_hot_down: bfloat16 [1280, 1792], P(('dp', 'pair'))
The draws below stay inside these ranges and needn't reach their ends.
Inputs may be any that keep to these rules, and one draw needn't show every extreme that they name: `expert_ids`: each token names 2 different experts; on every device at least 48 tokens name the hot expert, on some device all of them do, and some cold expert is named by 4 or more tokens. `route_slots`: on one device the routes to one expert carry the slots 0, 1, 2 and so on, each once. `hot_flags`: exactly one entry is 1. `owner_slot`: the cold experts hold the slots 0 to 63, each once; the hot expert's entry is 0.
All inputs are finite; a program needn't handle non-finite values.
Results may differ from the reference program's by a relative error of at most 0.0049.
Values may be sent and summed in bfloat16 or wider, within the bound.
A program may use at most 192 MiB of HBM per device.

```python
import jax
import jax.numpy as jnp
from jax import lax

D = 1792
FF = 1280
TOP = 2
TOK_DEV = 192
CAP = 4
HCAP = 48
COLD = 64
EXPERTS = 65
TOKENS = 24576
N_DP = 128


def shuffle_rows(key, length):
    return jax.random.permutation(key, length).astype(jnp.int32)


def rank_block(block_ids, block_prio):
    same = block_ids[:, None] == block_ids[None, :]
    earlier = block_prio[None, :] < block_prio[:, None]
    return jnp.sum(same & earlier, axis=1).astype(jnp.int32)


def routing(key):
    base = jax.random.fold_in(key, 4242)
    keys = jax.random.split(base, 7)
    order = jax.random.permutation(keys[0], EXPERTS).astype(jnp.int32)
    hot_id = order[0]
    busy_id = order[1]
    places = jnp.arange(EXPERTS, dtype=jnp.int32)
    ranks = jnp.zeros((EXPERTS,), jnp.int32).at[order].set(places)
    flags = (ranks == 0).astype(jnp.int32)
    cold_perm = jax.random.permutation(keys[1], COLD).astype(jnp.int32)
    owner = jnp.where(ranks == 0, 0, cold_perm[jnp.maximum(ranks - 1, 0)]).astype(jnp.int32)
    popular = jnp.where(ranks == 0, 0, 64 + 56 // jnp.maximum(ranks, 1)).astype(jnp.int32)
    device_keys = jax.random.split(keys[2], N_DP)
    position = jax.vmap(shuffle_rows, in_axes=(0, None))(device_keys, TOK_DEV).reshape(TOKENS)
    token_device = (jnp.arange(TOKENS, dtype=jnp.int32) // TOK_DEV).astype(jnp.int32)
    extra = jax.random.randint(keys[3], (TOKENS,), 0, 4) == 0
    hot_token = (position < HCAP) | extra | (token_device == 0)
    busy_token = position >= TOK_DEV - CAP
    raw_scores = jax.random.randint(keys[4], (TOKENS, EXPERTS), 0, 1024)
    scores = raw_scores * popular[None, :] * EXPERTS + places[None, :]
    scores = jnp.where(ranks[None, :] == 0, -1, scores)
    scores = jnp.where(busy_token[:, None] & (places[None, :] == busy_id), 1 << 30, scores)
    best = lax.top_k(scores, 2)[1].astype(jnp.int32)
    first = jnp.where(hot_token, hot_id, best[:, 0])
    second = jnp.where(hot_token, best[:, 0], best[:, 1])
    swapped = jax.random.randint(keys[5], (TOKENS,), 0, 2) == 1
    ids = jnp.stack([jnp.where(swapped, second, first), jnp.where(swapped, first, second)], axis=1).astype(jnp.int32)
    prio_keys = jax.random.split(keys[6], N_DP)
    priority = jax.vmap(shuffle_rows, in_axes=(0, None))(prio_keys, TOK_DEV * TOP)
    slots = jax.vmap(rank_block)(ids.reshape(N_DP, TOK_DEV * TOP), priority).reshape(TOKENS, TOP)
    return (ids, slots, flags, owner)


def draw_expert_ids(key, part):
    return routing(key)[0]


def draw_route_slots(key, part):
    return routing(key)[1]


def draw_hot_flags(key, part):
    return routing(key)[2]


def draw_owner_slot(key, part):
    return routing(key)[3]


def block_scale(own_key, extent, shards, low, top_value):
    level, own = 1.0, jax.random.fold_in(own_key, 6)
    for dim, parts in shards:
        draws = jnp.exp(jax.random.uniform(jax.random.fold_in(own, dim), (parts,), jnp.float32, low / len(shards), top_value / len(shards)))
        level = level * jnp.repeat(draws, extent[dim] // parts).reshape([-1 if axis == dim else 1 for axis in range(len(extent))])
    return level


def noise(rng, dims, width, bound, cuts=(), held_as=jnp.bfloat16):
    drawn = width * jax.random.normal(rng, dims, jnp.float32)
    if cuts:
        drawn = drawn * block_scale(rng, dims, cuts, -0.22, 0.18)
    return jnp.clip(drawn, -bound, bound).astype(held_as)


def setup_inputs(seed: int = 0) -> dict:
    splits = jax.random.split(jax.random.key(seed), 14)
    tokens = noise(splits[0], (TOKENS, D), 1.0, 6.0, ((0, 128),))
    grad_out = noise(splits[1], (TOKENS, D), 1.0, 6.0, ((0, 128),))
    gate_probs = jnp.clip(0.049804688 + 0.9501953 * jax.random.uniform(splits[2], (TOKENS, TOP), jnp.float32) ** block_scale(splits[2], (TOKENS, TOP), ((0, 128),), -0.2, 0.2), 0.049804688, 1.0).astype(jnp.bfloat16)
    expert_ids = draw_expert_ids(jax.random.fold_in(splits[13], 71), 0)
    route_slots = draw_route_slots(jax.random.fold_in(splits[13], 71), 0)
    hot_flags = draw_hot_flags(jax.random.fold_in(splits[13], 71), 0)
    owner_slot = draw_owner_slot(jax.random.fold_in(splits[13], 71), 0)
    cold_gate = noise(splits[7], (2 * COLD, FF // 2, D), D ** -0.5, 0.125, ((0, 128), (1, 2)))
    cold_up = noise(splits[8], (2 * COLD, FF // 2, D), D ** -0.5, 0.125, ((0, 128), (1, 2)))
    cold_down = noise(splits[9], (2 * COLD, FF // 2, D), FF ** -0.5, 0.15625, ((0, 128), (1, 2)))
    hot_gate = noise(splits[10], (FF, D), D ** -0.5, 0.125, ((0, 256),))
    hot_up = noise(splits[11], (FF, D), D ** -0.5, 0.125, ((0, 256),))
    hot_down = noise(splits[12], (FF, D), FF ** -0.5, 0.15625, ((0, 256),))
    return {"tokens": tokens, "grad_out": grad_out, "gate_probs": gate_probs, "expert_ids": expert_ids, "route_slots": route_slots, "hot_flags": hot_flags, "owner_slot": owner_slot, "cold_gate": cold_gate, "cold_up": cold_up, "cold_down": cold_down, "hot_gate": hot_gate, "hot_up": hot_up, "hot_down": hot_down}


def expert_back(rows_in, rows_grad, rows_gate, w_gate, w_up, w_down):
    pre_gate = jnp.dot(rows_in, w_gate.T, preferred_element_type=jnp.float32)
    pre_up = jnp.dot(rows_in, w_up.T, preferred_element_type=jnp.float32)
    back_proj = jnp.dot(rows_grad, w_down.T, preferred_element_type=jnp.float32)
    sigmoid_gate = 1.0 / (1.0 + jnp.exp(-pre_gate))
    activation = pre_gate * sigmoid_gate
    hidden = activation * pre_up
    prob_grad = jnp.sum(hidden * back_proj, axis=1)
    gate_scale = rows_gate.astype(jnp.float32)[:, None]
    hidden_grad = gate_scale * back_proj
    gate_grad = (hidden_grad * pre_up * sigmoid_gate * (1.0 + pre_gate * (1.0 - sigmoid_gate))).astype(jnp.bfloat16)
    up_grad = (hidden_grad * activation).astype(jnp.bfloat16)
    weighted = (gate_scale * hidden).astype(jnp.bfloat16)
    input_grad = jnp.dot(gate_grad, w_gate, preferred_element_type=jnp.float32) + jnp.dot(up_grad, w_up, preferred_element_type=jnp.float32)
    return gate_grad, up_grad, weighted, input_grad, prob_grad


def pick_rows(route_table, tokens, grad_out, flat_gate):
    token_index = (route_table // TOP).astype(jnp.int32)
    rows_in = jnp.take(tokens, token_index, axis=0, mode="fill", fill_value=0)
    rows_grad = jnp.take(grad_out, token_index, axis=0, mode="fill", fill_value=0)
    rows_gate = jnp.take(flat_gate, route_table, axis=0, mode="fill", fill_value=0)
    return token_index, rows_in, rows_grad, rows_gate


def weight_grads(gate_grad, up_grad, weighted, rows_in, rows_grad):
    grad_gate = jnp.dot(gate_grad.T, rows_in, preferred_element_type=jnp.float32).astype(jnp.bfloat16)
    grad_up = jnp.dot(up_grad.T, rows_in, preferred_element_type=jnp.float32).astype(jnp.bfloat16)
    grad_down = jnp.dot(weighted.T, rows_grad, preferred_element_type=jnp.float32).astype(jnp.bfloat16)
    return grad_gate, grad_up, grad_down


def reference(tokens, grad_out, gate_probs, expert_ids, route_slots, hot_flags, owner_slot, cold_gate, cold_up, cold_down, hot_gate, hot_up, hot_down):
    route_count = TOKENS * TOP
    flat_ids = expert_ids.reshape(-1)
    flat_slots = route_slots.reshape(-1)
    flat_gate = gate_probs.reshape(-1)
    routes = jnp.arange(route_count, dtype=jnp.int32)
    device = (routes // (TOK_DEV * TOP)).astype(jnp.int32)
    is_hot = hot_flags[flat_ids]
    owners = owner_slot[flat_ids]
    live_cold = (is_hot == 0) & (flat_slots < CAP)
    live_hot = (is_hot == 1) & (flat_slots < HCAP)
    cold_pos = jnp.where(live_cold, (owners * N_DP + device) * CAP + flat_slots, COLD * N_DP * CAP).astype(jnp.int32)
    cold_table = jnp.full((COLD * N_DP * CAP,), route_count, jnp.int32).at[cold_pos].set(routes, mode="drop")
    cold_table = cold_table.reshape(COLD, N_DP * CAP)
    hot_pos = jnp.where(live_hot, device * HCAP + flat_slots, N_DP * HCAP).astype(jnp.int32)
    hot_table = jnp.full((N_DP * HCAP,), route_count, jnp.int32).at[hot_pos].set(routes, mode="drop")

    def one_slot(slot_index):
        route_table = cold_table[slot_index]
        token_index, rows_in, rows_grad, rows_gate = pick_rows(route_table, tokens, grad_out, flat_gate)
        start_row = (2 * slot_index).astype(jnp.int32)
        w_gate = lax.dynamic_slice_in_dim(cold_gate, start_row, 2, 0).reshape(FF, D)
        w_up = lax.dynamic_slice_in_dim(cold_up, start_row, 2, 0).reshape(FF, D)
        w_down = lax.dynamic_slice_in_dim(cold_down, start_row, 2, 0).reshape(FF, D)
        gate_grad, up_grad, weighted, input_grad, prob_grad = expert_back(rows_in, rows_grad, rows_gate, w_gate, w_up, w_down)
        grad_gate, grad_up, grad_down = weight_grads(gate_grad, up_grad, weighted, rows_in, rows_grad)
        return input_grad, prob_grad, grad_gate.reshape(2, FF // 2, D), grad_up.reshape(2, FF // 2, D), grad_down.reshape(2, FF // 2, D)

    cold_dx, cold_dp, cold_gg, cold_gu, cold_gd = lax.map(one_slot, jnp.arange(COLD, dtype=jnp.int32))

    hot_tokens, hot_in, hot_grad, hot_rows_gate = pick_rows(hot_table, tokens, grad_out, flat_gate)
    gate_grad, up_grad, weighted, hot_dx, hot_dp = expert_back(hot_in, hot_grad, hot_rows_gate, hot_gate, hot_up, hot_down)
    grad_hot_gate, grad_hot_up, grad_hot_down = weight_grads(gate_grad, up_grad, weighted, hot_in, hot_grad)

    flat_cold = cold_table.reshape(-1)
    cold_tokens = (flat_cold // TOP).astype(jnp.int32)
    input_total = jnp.zeros((TOKENS, D), jnp.float32)
    input_total = input_total.at[cold_tokens].add(cold_dx.reshape(-1, D), mode="drop")
    input_total = input_total.at[hot_tokens].add(hot_dx, mode="drop")
    route_grad = jnp.zeros((route_count,), jnp.float32)
    route_grad = route_grad.at[flat_cold].add(cold_dp.reshape(-1), mode="drop")
    route_grad = route_grad.at[hot_table].add(hot_dp, mode="drop")
    return (input_total.astype(jnp.bfloat16), route_grad.reshape(TOKENS, TOP),
            cold_gg.reshape(2 * COLD, FF // 2, D), cold_gu.reshape(2 * COLD, FF // 2, D), cold_gd.reshape(2 * COLD, FF // 2, D),
            grad_hot_gate, grad_hot_up, grad_hot_down)
```

```python
import jax
import jax.numpy as jnp
from jax import lax
from jax.experimental import pallas as pl
from jax.experimental.pallas import tpu as pltpu
from jax.sharding import PartitionSpec as P

NX, NY, NZ = 4, 2, 8
CHIPS = NX * NY * NZ
RING = NY * NZ
CAP = 4
HCAP = 48
SIDE = 128
UNIT = 5
MESH = pl.DeviceIdType.MESH
F32 = jnp.float32
BF16 = jnp.bfloat16
VMEM = pltpu.VMEM
ROWS = (((0,), (0,)), ((), ()))
COLS = (((1,), (1,)), ((), ()))


def spec(space):
    return pl.BlockSpec(memory_space=space)


def params(**more):
    return pltpu.CompilerParams(vmem_limit_bytes=56 << 20, **more)


def iota(shape, axis):
    return lax.broadcasted_iota(jnp.int32, shape, axis)


def positions_kernel(flags, owner, ids, slots, out):
    chosen = ids[...]
    count = flags.shape[0]

    def step(entry, carry):
        hot, place = carry
        same = chosen == entry
        hot = jnp.where(same, flags[entry], hot)
        place = jnp.where(same, owner[entry], place)
        return hot, place

    zero = jnp.zeros(chosen.shape, jnp.int32)
    hot, place = lax.fori_loop(0, count, step, (zero, zero))
    slot = slots[...]
    cold_row = jnp.where(slot < CAP, place * CAP + slot, -1)
    hot_row = jnp.where(slot < HCAP, CHIPS * CAP + slot, -1)
    out[...] = jnp.where(hot == 1, hot_row, cold_row)


def cold_match(pos, low, rows, token_count):
    row = low + iota((rows, token_count), 0)
    within = row & 7
    return row, within, (row >> 3) * CAP + (within & 3)


def pack_kernel(flags, owner, ids, slots, probs, tokens, grad, gate, up, down, cold, hot, weights, pos):
    positions_kernel(flags, owner, ids, slots, pos)
    token_count, width = tokens.shape
    block = 8 * min(CHIPS, 16)
    gates = probs[...].astype(F32)

    def step(index, carry):
        low = pl.multiple_of(index * block, block)
        row, within, want = cold_match(pos, low, block, token_count)
        first = pos[0:1, :] == want
        second = pos[1:2, :] == want
        match = first | second
        pick_x = jnp.where(match & (within < CAP), 1.0, 0.0).astype(BF16)
        pick_g = jnp.where(match & (within >= CAP), 1.0, 0.0).astype(BF16)
        rows = jnp.dot(pick_x, tokens[...], preferred_element_type=F32)
        rows += jnp.dot(pick_g, grad[...], preferred_element_type=F32)
        cold[pl.ds(low, block), :width] = rows.astype(BF16)
        scale = jnp.where(first, gates[0:1, :], 0.0) + jnp.where(second, gates[1:2, :], 0.0)
        scale = jnp.sum(scale, axis=1, keepdims=True)
        cold[pl.ds(low, block), width:] = jnp.broadcast_to(scale, (block, SIDE)).astype(BF16)
        return carry

    lax.fori_loop(0, 8 * CHIPS // block, step, 0)
    want = CHIPS * CAP + iota((HCAP, token_count), 0)
    first = pos[0:1, :] == want
    second = pos[1:2, :] == want
    pick = jnp.where(first | second, 1.0, 0.0).astype(BF16)
    hot[:HCAP, :width] = jnp.dot(pick, tokens[...], preferred_element_type=F32).astype(BF16)
    hot[HCAP:, :width] = jnp.dot(pick, grad[...], preferred_element_type=F32).astype(BF16)
    scale = jnp.where(first, gates[0:1, :], 0.0) + jnp.where(second, gates[1:2, :], 0.0)
    scale = jnp.broadcast_to(jnp.sum(scale, axis=1, keepdims=True), (HCAP, SIDE)).astype(BF16)
    hot[:HCAP, width:] = scale
    hot[HCAP:, width:] = scale
    rest = jnp.zeros((16 - 3 * UNIT, width), F32)
    parts = [gate[...].astype(F32), up[...].astype(F32), down[...].astype(F32), rest]
    weights[...] = jnp.concatenate(parts, axis=0).astype(BF16)


def place():
    me = lax.axis_index("dp")
    core = lax.rem(me, 2)
    chip = lax.div(me, 2)
    return me, lax.axis_index("pair"), core, chip, lax.div(chip, RING), lax.rem(chip, RING)


def ring_shift(at, k):
    y, z = lax.div(at, NZ), lax.rem(at, NZ)
    return lax.rem(y + lax.div(k, NZ), NY) * NZ + lax.rem(z + lax.rem(k, NZ), NZ)


def remote(src, dst, send, recv, dp, pair):
    return pltpu.make_async_remote_copy(
        src_ref=src, dst_ref=dst, send_sem=send, recv_sem=recv, device_id=(dp, pair), device_id_type=MESH
    )


def greet(pair, core, x, at, sibling):
    barrier = pltpu.get_barrier_semaphore()

    def each(k, carry):
        chip = lax.rem(x + lax.div(k, RING), NX) * RING + ring_shift(at, lax.rem(k, RING))
        pl.semaphore_signal(barrier, inc=1, device_id=(chip * 2 + core, pair), device_id_type=MESH)
        return carry

    lax.fori_loop(1, CHIPS, each, 0)
    pl.semaphore_signal(barrier, inc=1, device_id=(sibling, pair), device_id_type=MESH)
    pl.semaphore_wait(barrier, CHIPS)


def spread_kernel(cold_in, hot_in, w_in, cold, hot, w, own, cold_send, hot_send, w_send, cold_recv, hot_recv, w_recv, side_send, side_recv):
    me, pair, core, chip, x, at = place()
    sibling = me + 1 - 2 * core
    mine = [
        pltpu.make_async_copy(cold_in.at[chip], cold.at[core, chip], own.at[0]),
        pltpu.make_async_copy(hot_in, hot.at[core, x], own.at[1]),
        pltpu.make_async_copy(w_in, w.at[at], own.at[2]),
    ]
    for copy in mine:
        copy.start()
    greet(pair, core, x, at, sibling)

    def send_w(k, carry):
        other = ring_shift(at, k)
        remote(w_in, w.at[at], w_send, w_recv, (x * RING + other) * 2 + core, pair).start()
        return carry

    lax.fori_loop(1, RING, send_w, 0)
    for j in range(1, NX):
        other = lax.rem(x + j, NX)
        remote(hot_in, hot.at[core, x], hot_send, hot_recv, (other * RING + at) * 2 + core, pair).start()
    for j in range(NX):

        def send_cold(k, carry, j=j):
            other = lax.rem(x + j, NX) * RING + ring_shift(at, k)
            remote(cold_in.at[other], cold.at[core, chip], cold_send, cold_recv.at[j], other * 2 + core, pair).start()
            return carry

        lax.fori_loop(1 if j == 0 else 0, RING, send_cold, 0)
    for copy in mine:
        copy.wait()

    remote(hot.at[core, pl.ds(0, NX - 1)], hot.at[core, pl.ds(0, NX - 1)], hot_send, hot_recv, sibling, pair).wait_recv()
    forward = [remote(hot.at[core], hot.at[core], side_send.at[NX], side_recv.at[NX], sibling, pair)]
    forward[0].start()
    for j in range(NX):
        source = lax.rem(x + NX - j, NX) * RING
        got = cold.at[core, pl.ds(source, RING - 1 if j == 0 else RING)]
        remote(got, got, cold_send, cold_recv.at[j], sibling, pair).wait_recv()
        block = cold.at[core, pl.ds(source, RING)]
        forward.append(remote(block, block, side_send.at[j], side_recv.at[j], sibling, pair))
        forward[-1].start()
    for copy in forward:
        copy.wait()
    remote(w.at[pl.ds(0, RING - 1)], w.at[pl.ds(0, RING - 1)], w_send, w_recv, sibling, pair).wait()
    remote(hot.at[core, pl.ds(0, NX - 1)], hot.at[core, pl.ds(0, NX - 1)], hot_send, hot_recv, sibling, pair).wait_send()
    sent = cold_in.at[pl.ds(0, CHIPS - 1)]
    remote(sent, sent, cold_send, cold_recv.at[0], sibling, pair).wait_send()


def swish(pre_gate, pre_up, back, scale):
    sigmoid = 1.0 / (1.0 + jnp.exp(-pre_gate))
    act = pre_gate * sigmoid
    hidden = act * pre_up
    probs = hidden * back
    hidden_grad = scale * back
    gate_grad = hidden_grad * pre_up * sigmoid * (1.0 + pre_gate * (1.0 - sigmoid))
    return gate_grad, hidden_grad * act, scale * hidden, probs


def work_kernel(cold, hot, w, c_gate, c_up, c_down, cold_out, hot_out, w_out, g_gate, g_up, g_down, d_gate, d_up, d_down, h_gate, h_down):
    width = c_gate.shape[1]
    half = width // 2
    rows = cold.shape[0]
    block = min(rows, 256)

    def cold_step(index, carry):
        at = pl.ds(pl.multiple_of(index * block, block), block)
        data = cold[at, :width]
        scale = cold[at, width : width + SIDE].astype(F32)[:, :1]
        pre_gate = lax.dot_general(data, c_gate[...], COLS, preferred_element_type=F32)
        pre_up = lax.dot_general(data, c_up[...], COLS, preferred_element_type=F32)
        back = lax.dot_general(data, c_down[...], COLS, preferred_element_type=F32)
        back = pltpu.roll(back, block - CAP, 0)
        gate_grad, up_grad, weighted, probs = swish(pre_gate, pre_up, back, scale)
        is_x = (iota(pre_gate.shape, 0) & 7) < CAP
        gate_grad = jnp.where(is_x, gate_grad, 0.0).astype(BF16)
        up_grad = jnp.where(is_x, up_grad, 0.0).astype(BF16)
        d_gate[at, :] = gate_grad
        d_up[at, :] = up_grad
        d_down[at, :] = pltpu.roll(jnp.where(is_x, weighted, 0.0), CAP, 0).astype(BF16)
        dx = jnp.dot(gate_grad, c_gate[...], preferred_element_type=F32)
        dx += jnp.dot(up_grad, c_up[...], preferred_element_type=F32)
        is_x = (iota((block, half), 0) & 7) < CAP
        packed = jnp.where(is_x, dx[:, :half], pltpu.roll(dx[:, half:], CAP, 0))
        cold_out[at, :half] = packed.astype(BF16)
        probs = jnp.sum(probs, axis=1, keepdims=True)
        cold_out[at, half:] = jnp.broadcast_to(probs, (block, SIDE)).astype(BF16)
        return carry

    lax.fori_loop(0, rows // block, cold_step, 0)
    step = 256
    for grads, out in ((d_gate, g_gate), (d_up, g_up), (d_down, g_down)):

        def grad_step(index, carry, grads=grads, out=out):
            at = pl.ds(pl.multiple_of(index * step, step), step)
            out[:, at] = lax.dot_general(grads[...], cold[:, at], ROWS, preferred_element_type=F32).astype(BF16)
            return carry

        lax.fori_loop(0, width // step, grad_step, 0)

    units = w.shape[0]
    lane = iota((HCAP, units), 1) & 15

    def hot_step(index, carry):
        both = pl.multiple_of(index * 2 * HCAP, 2 * HCAP)
        at = pl.ds(pl.multiple_of(index * HCAP, HCAP), HCAP)
        rows_in = hot[pl.ds(both, HCAP), :width]
        rows_grad = hot[pl.ds(both + HCAP, HCAP), :width]
        scale = hot[pl.ds(both, HCAP), width : width + SIDE].astype(F32)[:, :1]
        pre = lax.dot_general(rows_in, w[...], COLS, preferred_element_type=F32)
        back = lax.dot_general(rows_grad, w[...], COLS, preferred_element_type=F32)
        pre_up = pltpu.roll(pre, units - UNIT, 1)
        back = pltpu.roll(back, units - 2 * UNIT, 1)
        gate_grad, up_grad, weighted, probs = swish(pre, pre_up, back, scale)
        live = lane < UNIT
        up_grad = pltpu.roll(jnp.where(live, up_grad, 0.0), UNIT, 1)
        grads = (jnp.where(live, gate_grad, 0.0) + up_grad).astype(BF16)
        h_gate[pl.ds(both, HCAP), :] = grads
        h_gate[pl.ds(both + HCAP, HCAP), :] = pltpu.roll(jnp.where(live, weighted, 0.0), 2 * UNIT, 1).astype(BF16)
        hot_out[at, :width] = jnp.dot(grads, w[...], preferred_element_type=F32).astype(BF16)
        probs = jnp.sum(jnp.where(live, probs, 0.0), axis=1, keepdims=True)
        hot_out[at, width:] = jnp.broadcast_to(probs, (HCAP, SIDE)).astype(BF16)
        return carry

    lax.fori_loop(0, 2 * NX, hot_step, 0)

    def hot_grad_step(index, carry):
        at = pl.ds(pl.multiple_of(index * step, step), step)
        w_out[:, at] = lax.dot_general(h_gate[...], hot[:, at], ROWS, preferred_element_type=F32).astype(BF16)
        return carry

    lax.fori_loop(0, width // step, hot_grad_step, 0)


def collect_kernel(cold_in, hot_in, w_in, cold, hot, w, side_cold, side_hot, sum_cold, sum_hot, own, cold_send, hot_send, w_send, cold_recv, hot_recv, w_recv, side_send, side_recv):
    me, pair, core, chip, x, at = place()
    sibling = me + 1 - 2 * core
    keep = pltpu.make_async_copy(w_in.at[at], w.at[at], own.at[0])
    keep.start()
    greet(pair, core, x, at, sibling)
    aside = [remote(hot_in.at[1 - core], side_hot, side_send.at[NX], side_recv.at[NX], sibling, pair)]
    for j in range(NX):
        block = pl.ds(lax.rem(x + j, NX) * RING, RING)
        aside.append(remote(cold_in.at[1 - core, block], side_cold.at[block], side_send.at[j], side_recv.at[j], sibling, pair))
    for copy in aside:
        copy.start()

    def send_w(k, carry):
        other = ring_shift(at, k)
        remote(w_in.at[other], w.at[at], w_send, w_recv, (x * RING + other) * 2 + core, pair).start()
        return carry

    lax.fori_loop(1, RING, send_w, 0)

    aside[0].wait_recv()

    def add_hot(k, carry):
        sum_hot[k] = (hot_in[core, k].astype(F32) + side_hot[k].astype(F32)).astype(BF16)
        return carry

    lax.fori_loop(0, NX, add_hot, 0)
    for j in range(1, NX):
        other = lax.rem(x + j, NX)
        remote(sum_hot.at[other], hot.at[x], hot_send, hot_recv, (other * RING + at) * 2 + core, pair).start()
    mine = [pltpu.make_async_copy(sum_hot.at[x], hot.at[x], own.at[1])]
    mine[0].start()
    for j in range(NX):
        base = lax.rem(x + j, NX) * RING
        aside[1 + j].wait_recv()

        def add_cold(k, carry, base=base):
            other = base + k
            sum_cold[other] = (cold_in[core, other].astype(F32) + side_cold[other].astype(F32)).astype(BF16)
            return carry

        lax.fori_loop(0, RING, add_cold, 0)

        def send_cold(k, carry, base=base):
            other = base + ring_shift(at, k)
            remote(sum_cold.at[other], cold.at[chip], cold_send, cold_recv, other * 2 + core, pair).start()
            return carry

        lax.fori_loop(1 if j == 0 else 0, RING, send_cold, 0)
        if j == 0:
            mine.append(pltpu.make_async_copy(sum_cold.at[chip], cold.at[chip], own.at[2]))
            mine[1].start()
    for copy in aside:
        copy.wait_send()
    keep.wait()
    for copy in mine:
        copy.wait()
    for ref, send, recv, count in ((w, w_send, w_recv, RING - 1), (hot, hot_send, hot_recv, NX - 1), (cold, cold_send, cold_recv, CHIPS - 1)):
        part = ref.at[pl.ds(0, count)]
        remote(part, part, send, recv, sibling, pair).wait()


def unpack_kernel(pos, cold, hot, w, own_rows, other_rows, probs, g_gate, g_up, g_down, total):
    token_count = pos.shape[1]
    half = cold.shape[1] - SIDE
    width = 2 * half
    rows = cold.shape[0]
    mine = token_count // 2
    pair = lax.axis_index("pair")
    row, within, want = cold_match(pos, 0, rows, token_count)
    first = pos[0:1, :] == want
    second = pos[1:2, :] == want
    match = first | second
    pick_low = jnp.where(match & (within < CAP), 1.0, 0.0).astype(BF16)
    pick_high = jnp.where(match & (within >= CAP), 1.0, 0.0).astype(BF16)
    hot_rows = hot.shape[0]
    hot_want = CHIPS * CAP + lax.rem(iota((hot_rows, token_count), 0), HCAP)
    hot_first = pos[0:1, :] == hot_want
    hot_second = pos[1:2, :] == hot_want
    pick_hot = jnp.where(hot_first | hot_second, 1.0, 0.0).astype(BF16)
    for low, pick in ((0, pick_low), (half, pick_high)):
        part = lax.dot_general(pick, cold[:, :half], ROWS, preferred_element_type=F32)
        part += lax.dot_general(pick_hot, hot[:, low : low + half], ROWS, preferred_element_type=F32)
        total[:, low : low + half] = part
    own_rows[...] = total[pl.ds(pl.multiple_of(pair * mine, 8), mine), :]
    other_rows[...] = total[pl.ds(pl.multiple_of((1 - pair) * mine, 8), mine), :].astype(BF16)
    cold_probs = cold[:, half:].astype(F32)[:, :1]
    hot_probs = hot[:, width:].astype(F32)[:, :1]
    is_x = within < CAP
    for k, (a, b) in enumerate(((first, hot_first), (second, hot_second))):
        value = jnp.sum(jnp.where(a & is_x, cold_probs, 0.0), axis=0, keepdims=True)
        value += jnp.sum(jnp.where(b, hot_probs, 0.0), axis=0, keepdims=True)
        probs[k : k + 1, :] = value
    grads = w[0].astype(F32)
    for k in range(1, w.shape[0]):
        grads += w[k].astype(F32)
    g_gate[...] = grads[0:UNIT].astype(BF16)
    g_up[...] = grads[UNIT : 2 * UNIT].astype(BF16)
    g_down[...] = grads[2 * UNIT : 3 * UNIT].astype(BF16)


def shape(*dims, dtype=BF16):
    return jax.ShapeDtypeStruct(dims, dtype)


def local(tokens, grad_out, gate_probs, expert_ids, route_slots, hot_flags, owner_slot, cold_gate, cold_up, cold_down, hot_gate, hot_up, hot_down):
    token_count, width = tokens.shape
    wide, half = width + SIDE, width // 2
    ff = cold_gate.shape[1]
    units = 16 * RING
    dma = pltpu.SemaphoreType.DMA
    cold, hot, weights, pos = pl.pallas_call(
        pack_kernel,
        out_shape=(shape(8 * CHIPS, wide), shape(2 * HCAP, wide), shape(16, width), shape(2, token_count, dtype=jnp.int32)),
        in_specs=[spec(pltpu.SMEM)] * 2 + [spec(VMEM)] * 8,
        out_specs=[spec(VMEM)] * 4,
        compiler_params=params(),
    )(hot_flags, owner_slot, expert_ids.T, route_slots.T, gate_probs.T, tokens, grad_out, hot_gate, hot_up, hot_down)

    got_cold, got_hot, got_w = pl.pallas_call(
        spread_kernel,
        out_shape=(shape(2, CHIPS, 8, wide), shape(2, NX, 2 * HCAP, wide), shape(RING, 16, width)),
        in_specs=[spec(pl.ANY)] * 3,
        out_specs=[spec(pl.ANY)] * 3,
        scratch_shapes=[dma((3,)), dma, dma, dma, dma((NX,)), dma, dma, dma((NX + 1,)), dma((NX + 1,))],
        compiler_params=params(collective_id=0, has_side_effects=True),
    )(cold.reshape(CHIPS, 8, wide), hot, weights)

    ret_cold, ret_hot, ret_w, g_gate, g_up, g_down = pl.pallas_call(
        work_kernel,
        out_shape=(shape(16 * CHIPS, half + SIDE), shape(2 * NX * HCAP, wide), shape(units, width)) + (shape(ff, width),) * 3,
        in_specs=[spec(VMEM)] * 6,
        out_specs=[spec(VMEM)] * 6,
        scratch_shapes=[VMEM((16 * CHIPS, ff), BF16)] * 3 + [VMEM((4 * NX * HCAP, units), BF16)] * 2,
        compiler_params=params(),
    )(got_cold.reshape(16 * CHIPS, wide), got_hot.reshape(4 * NX * HCAP, wide), got_w.reshape(units, width), cold_gate[0], cold_up[0], cold_down[0])

    back_cold, back_hot, back_w = pl.pallas_call(
        collect_kernel,
        out_shape=(shape(CHIPS, 8, half + SIDE), shape(NX, HCAP, wide), shape(RING, 16, width)),
        in_specs=[spec(VMEM), spec(VMEM), spec(pl.ANY)],
        out_specs=[spec(pl.ANY)] * 3,
        scratch_shapes=[
            VMEM((CHIPS, 8, half + SIDE), BF16),
            VMEM((NX, HCAP, wide), BF16),
            VMEM((CHIPS, 8, half + SIDE), BF16),
            VMEM((NX, HCAP, wide), BF16),
            dma((3,)), dma, dma, dma, dma, dma, dma, dma((NX + 1,)), dma((NX + 1,)),
        ],
        compiler_params=params(collective_id=1, has_side_effects=True),
    )(ret_cold.reshape(2, CHIPS, 8, half + SIDE), ret_hot.reshape(2, NX, HCAP, wide), ret_w.reshape(RING, 16, width))

    mine = token_count // 2
    own_rows, other_rows, probs, h_gate, h_up, h_down = pl.pallas_call(
        unpack_kernel,
        out_shape=(shape(mine, width, dtype=F32), shape(mine, width), shape(2, token_count, dtype=F32)) + (shape(UNIT, width),) * 3,
        in_specs=[spec(VMEM)] * 4,
        out_specs=[spec(VMEM)] * 6,
        scratch_shapes=[VMEM((token_count, width), F32)],
        compiler_params=params(),
    )(pos, back_cold.reshape(8 * CHIPS, half + SIDE), back_hot.reshape(NX * HCAP, wide), back_w)

    swap = [(0, 1), (1, 0)]
    pair = lax.axis_index("pair")
    halves = probs.T.reshape(2, mine, 2)
    own_probs = jnp.where(pair == 0, halves[0], halves[1])
    other_probs = jnp.where(pair == 0, halves[1], halves[0])
    summed = own_rows + lax.ppermute(other_rows, "pair", swap).astype(F32)
    summed_probs = own_probs + lax.ppermute(other_probs, "pair", swap)
    return (summed.astype(BF16), summed_probs, g_gate[None], g_up[None], g_down[None], h_gate, h_up, h_down)


def solution(mesh):
    split = P(("dp", "pair"), None)
    cold = P("dp", "pair", None)
    return jax.shard_map(
        local,
        mesh=mesh,
        in_specs=(P("dp", None),) * 5 + (P(), P()) + (cold,) * 3 + (split,) * 3,
        out_specs=(split, split, cold, cold, cold, split, split, split),
        check_vma=False,
    )
```

```python
import jax
import jax.numpy as jnp
from jax import lax
from jax.experimental import pallas as pl
from jax.experimental.pallas import tpu as pltpu
from jax.sharding import PartitionSpec as P

NX, NY, NZ = 4, 2, 8
CHIPS = NX * NY * NZ
RING = NY * NZ
CAP = 4
HCAP = 48
SIDE = 128
UNIT = 5
GROUPS = NX * NY // 2
MESH = pl.DeviceIdType.MESH
F32 = jnp.float32
BF16 = jnp.bfloat16
VMEM = pltpu.VMEM
ROWS = (((0,), (0,)), ((), ()))
COLS = (((1,), (1,)), ((), ()))


def spec(space):
    return pl.BlockSpec(memory_space=space)


def params(**more):
    return pltpu.CompilerParams(vmem_limit_bytes=56 << 20, **more)


def iota(shape, axis):
    return lax.broadcasted_iota(jnp.int32, shape, axis)


def positions_kernel(flags, owner, ids, slots, out):
    chosen = ids[...]
    count = flags.shape[0]

    def step(entry, carry):
        hot, place = carry
        same = chosen == entry
        hot = jnp.where(same, flags[entry], hot)
        place = jnp.where(same, owner[entry], place)
        return hot, place

    zero = jnp.zeros(chosen.shape, jnp.int32)
    hot, place = lax.fori_loop(0, count, step, (zero, zero))
    slot = slots[...]
    cold_row = jnp.where(slot < CAP, place * CAP + slot, -1)
    hot_row = jnp.where(slot < HCAP, CHIPS * CAP + slot, -1)
    out[...] = jnp.where(hot == 1, hot_row, cold_row)


def cold_match(pos, low, rows, token_count):
    row = low + iota((rows, token_count), 0)
    within = row & 7
    return row, within, (row >> 3) * CAP + (within & 3)


def pack_kernel(flags, owner, ids, slots, probs, tokens, grad, gate, up, down, cold, hot_x, hot_g, weights, pos):
    positions_kernel(flags, owner, ids, slots, pos)
    token_count, width = tokens.shape
    block = 8 * min(CHIPS, 16)
    gates = probs[...].astype(F32)

    def step(index, carry):
        low = pl.multiple_of(index * block, block)
        row, within, want = cold_match(pos, low, block, token_count)
        first = pos[0:1, :] == want
        second = pos[1:2, :] == want
        match = first | second
        pick_x = jnp.where(match & (within < CAP), 1.0, 0.0).astype(BF16)
        pick_g = jnp.where(match & (within >= CAP), 1.0, 0.0).astype(BF16)
        rows = jnp.dot(pick_x, tokens[...], preferred_element_type=F32)
        rows += jnp.dot(pick_g, grad[...], preferred_element_type=F32)
        cold[pl.ds(low, block), :width] = rows.astype(BF16)
        scale = jnp.where(first, gates[0:1, :], 0.0) + jnp.where(second, gates[1:2, :], 0.0)
        scale = jnp.sum(scale, axis=1, keepdims=True)
        cold[pl.ds(low, block), width:] = jnp.broadcast_to(scale, (block, SIDE)).astype(BF16)
        return carry

    lax.fori_loop(0, 8 * CHIPS // block, step, 0)
    want = CHIPS * CAP + iota((HCAP, token_count), 0)
    first = pos[0:1, :] == want
    second = pos[1:2, :] == want
    pick = jnp.where(first | second, 1.0, 0.0).astype(BF16)
    hot_x[:, :width] = jnp.dot(pick, tokens[...], preferred_element_type=F32).astype(BF16)
    hot_g[...] = jnp.dot(pick, grad[...], preferred_element_type=F32).astype(BF16)
    scale = jnp.where(first, gates[0:1, :], 0.0) + jnp.where(second, gates[1:2, :], 0.0)
    hot_x[:, width:] = jnp.broadcast_to(jnp.sum(scale, axis=1, keepdims=True), (HCAP, SIDE)).astype(BF16)
    rest = jnp.zeros((16 - 3 * UNIT, width), F32)
    parts = [gate[...].astype(F32), up[...].astype(F32), down[...].astype(F32), rest]
    weights[...] = jnp.concatenate(parts, axis=0).astype(BF16)


def place():
    me = lax.axis_index("dp")
    core = lax.rem(me, 2)
    chip = lax.div(me, 2)
    ring = lax.rem(chip, RING)
    return lax.axis_index("pair"), core, lax.div(chip, RING), lax.div(ring, NZ), lax.rem(ring, NZ)


def device(x, y, z, core, pair):
    return (((x * NY + y) * NZ + z) * 2 + core, pair)


def remote(src, dst, send, recv, to):
    return pltpu.make_async_remote_copy(
        src_ref=src, dst_ref=dst, send_sem=send, recv_sem=recv, device_id=to, device_id_type=MESH
    )


def swish(pre_gate, pre_up, back, scale):
    sigmoid = 1.0 / (1.0 + jnp.exp(-pre_gate))
    act = pre_gate * sigmoid
    hidden = act * pre_up
    probs = hidden * back
    hidden_grad = scale * back
    gate_grad = hidden_grad * pre_up * sigmoid * (1.0 + pre_gate * (1.0 - sigmoid))
    return gate_grad, hidden_grad * act, scale * hidden, probs


def layer_kernel(
    cold_in, hot_x_in, hot_g_in, w_in, c_gate, c_up, c_down,
    back_cold, back_hot, back_w, g_gate, g_up, g_down,
    cold, hot_x, hot_g, w, d_gate, d_up, d_down, d_hot, ret, away, side, pass_on, passed, final,
    hot_ret, hot_away, hot_side, hot_sum, w_ret,
    own, cold_send, cold_recv, hot_send, hot_recv, w_send, w_recv, near_send, near_recv, over_send, over_recv,
    side_send, side_recv, pass_send, pass_recv, back_send, back_recv, hb_send, hb_recv, wb_send, wb_recv, one_send,
):
    width = c_gate.shape[1]
    half = width // 2
    pair, core, x, y, z = place()
    sibling = device(x, y, z, 1 - core, pair)
    partner = device(x, y, z, core, 1 - pair)

    def along(kx, ky, kz):
        other_y = lax.rem(y + ky, NY)
        other_pair = lax.rem(pair + ky, 2)
        return device(lax.rem(x + kx, NX), other_y, lax.rem(z + kz, NZ), core, other_pair)

    barrier = pltpu.get_barrier_semaphore()

    def greet(k, carry):
        to = along(lax.div(k, RING), lax.div(lax.rem(k, RING), NZ), lax.rem(k, NZ))
        pl.semaphore_signal(barrier, inc=1, device_id=to, device_id_type=MESH)
        return carry

    lax.fori_loop(1, CHIPS, greet, 0)
    pl.semaphore_signal(barrier, inc=1, device_id=sibling, device_id_type=MESH)
    pl.semaphore_signal(barrier, inc=1, device_id=partner, device_id_type=MESH)
    pl.semaphore_wait(barrier, CHIPS + 1)

    def hot_at(which, k):
        return pl.ds(pl.multiple_of((which * NX + k) * HCAP, HCAP), HCAP)

    mine = [
        pltpu.make_async_copy(hot_x_in, hot_x.at[hot_at(core, 0)], own.at[0]),
        pltpu.make_async_copy(hot_g_in, hot_g.at[hot_at(core, 0)], own.at[1]),
        pltpu.make_async_copy(w_in, w.at[pl.ds(0, 16)], own.at[2]),
    ]
    for copy in mine:
        copy.start()
    for k in range(1, NX):
        remote(hot_x_in, hot_x.at[hot_at(core, k)], hot_send.at[0], hot_recv.at[0], along(k, 0, 0)).start()
        remote(hot_g_in, hot_g.at[hot_at(core, k)], hot_send.at[1], hot_recv.at[1], along(k, 0, 0)).start()

    def send_w(k, carry):
        slot = pl.ds(pl.multiple_of(k * 16, 16), 16)
        remote(w_in, w.at[slot], w_send, w_recv, along(0, lax.div(k, NZ), lax.rem(k, NZ))).start()
        return carry

    lax.fori_loop(1, RING, send_w, 0)

    def cold_at(group, which):
        return pl.ds((group * 2 + which) * NZ, NZ)

    for j in range(GROUPS):
        kx, ky = pair + 2 * (j // NY), j % NY
        to_x, to_y = lax.rem(x + kx, NX), lax.rem(y + ky, NY)

        def cold_copy(kz, j=j, kx=kx, ky=ky, to_x=to_x, to_y=to_y):
            chip = (to_x * NY + to_y) * NZ + lax.rem(z + kz, NZ)
            slot = (j * 2 + core) * NZ + z
            return cold_in.at[chip], cold.at[slot], along(kx, ky, kz)

        if j == 0:
            src, dst, to = cold_copy(0)

            @pl.when(pair == 0)
            def _():
                pltpu.make_async_copy(src, dst, cold_recv.at[0]).start()

            @pl.when(pair == 1)
            def _():
                remote(src, dst, one_send.at[0], cold_recv.at[0], to).start()

        def send_cold(kz, carry, j=j, cold_copy=cold_copy):
            src, dst, to = cold_copy(kz)
            remote(src, dst, cold_send, cold_recv.at[j], to).start()
            return carry

        lax.fori_loop(1 if j == 0 else 0, NZ, send_cold, 0)

    started = []

    def start(copy):
        copy.start()
        started.append(copy)
        return copy

    mine[0].wait()
    mine[1].wait()
    others = pl.ds(0, (NX - 1) * HCAP)
    remote(hot_x.at[others], hot_x.at[others], hot_send.at[0], hot_recv.at[0], sibling).wait_recv()
    remote(hot_g.at[others], hot_g.at[others], hot_send.at[1], hot_recv.at[1], sibling).wait_recv()
    this = pl.ds(pl.multiple_of(core * NX * HCAP, HCAP), NX * HCAP)
    hot_over = [
        start(remote(hot_x.at[this], hot_x.at[this], over_send.at[2 * GROUPS], over_recv.at[2 * GROUPS], sibling)),
        start(remote(hot_g.at[this], hot_g.at[this], over_send.at[2 * GROUPS + 1], over_recv.at[2 * GROUPS + 1], sibling)),
    ]
    mine[2].wait()
    w_others = pl.ds(0, (RING - 1) * 16)
    remote(w.at[w_others], w.at[w_others], w_send, w_recv, sibling).wait_recv()
    for copy in hot_over:
        copy.wait_recv()

    units = w.shape[0]
    hot_rows = hot_x.shape[0]
    lane = iota((hot_rows, units), 1) & 15
    scale = hot_x[:, width : width + SIDE].astype(F32)[:, :1]
    pre = lax.dot_general(hot_x[:, :width], w[...], COLS, preferred_element_type=F32)
    project = lax.dot_general(hot_g[...], w[...], COLS, preferred_element_type=F32)
    pre_up = pltpu.roll(pre, units - UNIT, 1)
    project = pltpu.roll(project, units - 2 * UNIT, 1)
    gate_grad, up_grad, weighted, probs = swish(pre, pre_up, project, scale)
    live = lane < UNIT
    up_grad = pltpu.roll(jnp.where(live, up_grad, 0.0), UNIT, 1)
    grads = (jnp.where(live, gate_grad, 0.0) + up_grad).astype(BF16)
    d_hot[:hot_rows, :] = grads
    d_hot[hot_rows:, :] = pltpu.roll(jnp.where(live, weighted, 0.0), 2 * UNIT, 1).astype(BF16)
    hot_ret[:, :width] = jnp.dot(grads, w[...], preferred_element_type=F32)
    probs = jnp.sum(jnp.where(live, probs, 0.0), axis=1, keepdims=True)
    hot_ret[:, width:] = jnp.broadcast_to(probs, (hot_rows, SIDE))
    that = pl.ds(pl.multiple_of((1 - core) * NX * HCAP, HCAP), NX * HCAP)
    hot_away[...] = hot_ret[that, :].astype(BF16)
    hot_swap = start(remote(hot_away, hot_side, side_send.at[2 * GROUPS], side_recv.at[2 * GROUPS], sibling))
    w_grad = lax.dot_general(d_hot[:hot_rows, :], hot_x[:, :width], ROWS, preferred_element_type=F32)
    w_grad += lax.dot_general(d_hot[hot_rows:, :], hot_g[...], ROWS, preferred_element_type=F32)
    w_ret[...] = w_grad.astype(BF16)

    def back(kx, ky, kz):
        return along(lax.rem(NX - kx, NX), ky, NZ - kz)

    def return_w(k, carry):
        slot = pl.ds(pl.multiple_of(k * 16, 16), 16)
        to = back(0, lax.div(k, NZ), lax.rem(k, NZ))
        remote(w_ret.at[slot], back_w.at[k], wb_send, wb_recv, to).start()
        return carry

    lax.fori_loop(1, RING, return_w, 0)
    mine = [pltpu.make_async_copy(w_ret.at[pl.ds(0, 16)], back_w.at[0], own.at[0])]
    mine[0].start()

    near, over = [], []

    def hand_over(group):
        ref = cold.at[cold_at(group, core)]
        over.append(start(remote(ref, ref, over_send.at[group], over_recv.at[group], sibling)))

    for j in range(GROUPS):
        ref = cold.at[cold_at(j, core)]
        remote(ref, ref, cold_send, cold_recv.at[j], sibling).wait_recv()
        to = cold.at[cold_at(GROUPS + j, core)]
        near.append(start(remote(ref, to, near_send.at[j], near_recv.at[j], partner)))
        hand_over(j)
    hot_swap.wait_recv()
    for k in range(NX):
        at = pl.ds(k * HCAP, HCAP)
        source = pl.ds(pl.multiple_of((core * NX + k) * HCAP, HCAP), HCAP)
        hot_sum[at, :] = (hot_ret[source, :] + hot_side[at, :].astype(F32)).astype(BF16)
        if k:
            remote(hot_sum.at[at], back_hot.at[k], hb_send, hb_recv, back(k, 0, 0)).start()
        else:
            mine.append(pltpu.make_async_copy(hot_sum.at[at], back_hot.at[0], own.at[1]))
            mine[1].start()
    for j in range(GROUPS):
        near[j].wait_recv()
        hand_over(GROUPS + j)

    block = 4 * 8 * NZ
    side_copies = {}

    def compute(index):
        for group in (2 * index, 2 * index + 1):
            over[group].wait_recv()
        at = slice(index * block, (index + 1) * block)
        data = cold[index * 4 * NZ : (index + 1) * 4 * NZ].reshape(block, width + SIDE)
        scale = data[:, width:].astype(F32)[:, :1]
        data = data[:, :width]
        pre_gate = lax.dot_general(data, c_gate[...], COLS, preferred_element_type=F32)
        pre_up = lax.dot_general(data, c_up[...], COLS, preferred_element_type=F32)
        project = lax.dot_general(data, c_down[...], COLS, preferred_element_type=F32)
        project = pltpu.roll(project, block - CAP, 0)
        gate_grad, up_grad, weighted, probs = swish(pre_gate, pre_up, project, scale)
        is_x = (iota(pre_gate.shape, 0) & 7) < CAP
        gate_grad = jnp.where(is_x, gate_grad, 0.0).astype(BF16)
        up_grad = jnp.where(is_x, up_grad, 0.0).astype(BF16)
        d_gate[at, :] = gate_grad
        d_up[at, :] = up_grad
        d_down[at, :] = pltpu.roll(jnp.where(is_x, weighted, 0.0), CAP, 0).astype(BF16)
        dx = jnp.dot(gate_grad, c_gate[...], preferred_element_type=F32)
        dx += jnp.dot(up_grad, c_up[...], preferred_element_type=F32)
        is_x = (iota((block, half), 0) & 7) < CAP
        ret[at, :half] = jnp.where(is_x, dx[:, :half], pltpu.roll(dx[:, half:], CAP, 0))
        probs = jnp.sum(probs, axis=1, keepdims=True)
        ret[at, half:] = jnp.broadcast_to(probs, (block, SIDE))
        for group in (2 * index, 2 * index + 1):
            away[group] = ret[rows_of(group, 1 - core), :].astype(BF16)
            side_copies[group] = start(remote(away.at[group], side.at[group], side_send.at[group], side_recv.at[group], sibling))

    def rows_of(group, which):
        return pl.ds(pl.multiple_of((group * 2 + which) * 8 * NZ, 8 * NZ), 8 * NZ)

    passes = {}

    def summed(group):
        side_copies[group].wait_recv()
        return ret[rows_of(group, core), :] + side[group].astype(F32)

    def pass_over(j):
        pass_on[j] = summed(GROUPS + j).astype(BF16)
        passes[j] = start(remote(pass_on.at[j], passed.at[j], pass_send.at[j], pass_recv.at[j], partner))

    def give_back(j):
        passes[j].wait_recv()
        value = (summed(j) + passed[j].astype(F32)).astype(BF16)
        final[j * NZ : (j + 1) * NZ] = value.reshape(NZ, 8, half + SIDE)
        ky = j % NY
        kx = lax.rem(pair + ky, 2) + 2 * (j // NY)

        def back_copy(kz):
            source = lax.rem(z + NZ - kz, NZ)
            return final.at[j * NZ + source], back_cold.at[j * NZ + z], back(kx, ky, kz)

        if j == 0:
            src, dst, to = back_copy(0)

            @pl.when(pair == 0)
            def _():
                pltpu.make_async_copy(src, dst, back_recv).start()

            @pl.when(pair == 1)
            def _():
                remote(src, dst, one_send.at[1], back_recv, to).start()

        def send_back(kz, carry):
            src, dst, to = back_copy(kz)
            remote(src, dst, back_send, back_recv, to).start()
            return carry

        lax.fori_loop(1 if j == 0 else 0, NZ, send_back, 0)

    def weight_grad(grads, out):
        data = cold[...].reshape(cold.shape[0] * 8, width + SIDE)[:, :width]
        out[...] = lax.dot_general(grads[...], data, ROWS, preferred_element_type=F32).astype(BF16)

    pairs = GROUPS // 2
    for index in range(pairs):
        compute(index)
        if index:
            give_back(2 * index - 2)
            give_back(2 * index - 1)
        compute(pairs + index)
        pass_over(2 * index)
        pass_over(2 * index + 1)
    weight_grad(d_gate, g_gate)
    give_back(GROUPS - 2)
    give_back(GROUPS - 1)
    weight_grad(d_up, g_up)
    weight_grad(d_down, g_down)

    for copy in started:
        copy.wait_send()
    for copy in mine:
        copy.wait()
    for part, send, recv in (
        (hot_x.at[others], hot_send.at[0], None),
        (hot_g.at[others], hot_send.at[1], None),
        (w.at[w_others], w_send, None),
        (cold_in.at[pl.ds(0, GROUPS * NZ - 1)], cold_send, None),
        (final.at[pl.ds(0, GROUPS * NZ - 1)], back_send, None),
        (back_w.at[pl.ds(0, RING - 1)], wb_send, wb_recv),
        (back_hot.at[pl.ds(0, NX - 1)], hb_send, hb_recv),
    ):
        remote(part, part, send, own.at[0] if recv is None else recv, sibling).wait_send()
        if recv is not None:
            remote(part, part, send, recv, sibling).wait_recv()
    remote(back_cold, back_cold, back_send, back_recv, sibling).wait_recv()

    @pl.when(pair == 1)
    def _():
        remote(cold_in.at[0], cold_in.at[0], one_send.at[0], back_recv, sibling).wait_send()
        remote(final.at[0], final.at[0], one_send.at[1], back_recv, sibling).wait_send()


def unpack_kernel(pos, cold, hot, w, own_rows, other_rows, probs, g_gate, g_up, g_down, total):
    token_count = pos.shape[1]
    half = cold.shape[1] - SIDE
    width = 2 * half
    rows = cold.shape[0]
    mine = token_count // 2
    pair, _, x, y, _ = place()
    row = iota((rows, token_count), 0)
    within = row & 7
    group = lax.div(row, 8 * NZ)
    owner_x = lax.rem(x + pair + 2 * lax.div(group, NY), NX)
    owner_y = lax.rem(y + lax.rem(group, NY), NY)
    owner = (owner_x * NY + owner_y) * NZ + lax.rem(lax.div(row, 8), NZ)
    want = owner * CAP + (within & 3)
    first = pos[0:1, :] == want
    second = pos[1:2, :] == want
    match = first | second
    pick_low = jnp.where(match & (within < CAP), 1.0, 0.0).astype(BF16)
    pick_high = jnp.where(match & (within >= CAP), 1.0, 0.0).astype(BF16)
    hot_rows = hot.shape[0]
    hot_want = CHIPS * CAP + lax.rem(iota((hot_rows, token_count), 0), HCAP)
    hot_first = pos[0:1, :] == hot_want
    hot_second = pos[1:2, :] == hot_want
    pick_hot = jnp.where(hot_first | hot_second, 1.0, 0.0).astype(BF16)
    for low, pick in ((0, pick_low), (half, pick_high)):
        part = lax.dot_general(pick, cold[:, :half], ROWS, preferred_element_type=F32)
        part += lax.dot_general(pick_hot, hot[:, low : low + half], ROWS, preferred_element_type=F32)
        total[:, low : low + half] = part
    own_rows[...] = total[pl.ds(pl.multiple_of(pair * mine, 8), mine), :]
    other_rows[...] = total[pl.ds(pl.multiple_of((1 - pair) * mine, 8), mine), :].astype(BF16)
    cold_probs = cold[:, half:].astype(F32)[:, :1]
    hot_probs = hot[:, width:].astype(F32)[:, :1]
    is_x = within < CAP
    for k, (a, b) in enumerate(((first, hot_first), (second, hot_second))):
        value = jnp.sum(jnp.where(a & is_x, cold_probs, 0.0), axis=0, keepdims=True)
        value += jnp.sum(jnp.where(b, hot_probs, 0.0), axis=0, keepdims=True)
        probs[k : k + 1, :] = value
    grads = w[0].astype(F32)
    for k in range(1, w.shape[0]):
        grads += w[k].astype(F32)
    g_gate[...] = grads[0:UNIT].astype(BF16)
    g_up[...] = grads[UNIT : 2 * UNIT].astype(BF16)
    g_down[...] = grads[2 * UNIT : 3 * UNIT].astype(BF16)


def shape(*dims, dtype=BF16):
    return jax.ShapeDtypeStruct(dims, dtype)


def local(tokens, grad_out, gate_probs, expert_ids, route_slots, hot_flags, owner_slot, cold_gate, cold_up, cold_down, hot_gate, hot_up, hot_down):
    token_count, width = tokens.shape
    wide, half = width + SIDE, width // 2
    ff = cold_gate.shape[1]
    units = 16 * RING
    dma = pltpu.SemaphoreType.DMA
    cold, hot_x, hot_g, weights, pos = pl.pallas_call(
        pack_kernel,
        out_shape=(shape(8 * CHIPS, wide), shape(HCAP, wide), shape(HCAP, width), shape(16, width), shape(2, token_count, dtype=jnp.int32)),
        in_specs=[spec(pltpu.SMEM)] * 2 + [spec(VMEM)] * 8,
        out_specs=[spec(VMEM)] * 5,
        compiler_params=params(),
    )(hot_flags, owner_slot, expert_ids.T, route_slots.T, gate_probs.T, tokens, grad_out, hot_gate, hot_up, hot_down)

    packed = half + SIDE
    lines = 8 * NZ
    hot_rows = 2 * NX * HCAP
    back_cold, back_hot, back_w, g_gate, g_up, g_down = pl.pallas_call(
        layer_kernel,
        out_shape=(shape(GROUPS * NZ, 8, packed), shape(NX, HCAP, wide), shape(RING, 16, width)) + (shape(ff, width),) * 3,
        in_specs=[spec(pl.ANY)] * 4 + [spec(VMEM)] * 3,
        out_specs=[spec(pl.ANY)] * 3 + [spec(VMEM)] * 3,
        scratch_shapes=[
            VMEM((2 * CHIPS, 8, wide), BF16), VMEM((hot_rows, wide), BF16), VMEM((hot_rows, width), BF16), VMEM((units, width), BF16),
            VMEM((16 * CHIPS, ff), BF16), VMEM((16 * CHIPS, ff), BF16), VMEM((16 * CHIPS, ff), BF16), VMEM((2 * hot_rows, units), BF16),
            VMEM((16 * CHIPS, packed), F32), VMEM((2 * GROUPS, lines, packed), BF16), VMEM((2 * GROUPS, lines, packed), BF16),
            VMEM((GROUPS, lines, packed), BF16), VMEM((GROUPS, lines, packed), BF16), VMEM((GROUPS * NZ, 8, packed), BF16),
            VMEM((hot_rows, wide), F32), VMEM((NX * HCAP, wide), BF16), VMEM((NX * HCAP, wide), BF16), VMEM((NX * HCAP, wide), BF16), VMEM((units, width), BF16),
            dma((3,)), dma, dma((GROUPS,)), dma((2,)), dma((2,)), dma, dma, dma((GROUPS,)), dma((GROUPS,)),
            dma((2 * GROUPS + 2,)), dma((2 * GROUPS + 2,)), dma((2 * GROUPS + 1,)), dma((2 * GROUPS + 1,)),
            dma((GROUPS,)), dma((GROUPS,)), dma, dma, dma, dma, dma, dma, dma((2,)),
        ],
        compiler_params=params(collective_id=0, has_side_effects=True),
    )(cold.reshape(CHIPS, 8, wide), hot_x, hot_g, weights, cold_gate[0], cold_up[0], cold_down[0])

    mine = token_count // 2
    own_rows, other_rows, probs, h_gate, h_up, h_down = pl.pallas_call(
        unpack_kernel,
        out_shape=(shape(mine, width, dtype=F32), shape(mine, width), shape(2, token_count, dtype=F32)) + (shape(UNIT, width),) * 3,
        in_specs=[spec(VMEM)] * 4,
        out_specs=[spec(VMEM)] * 6,
        scratch_shapes=[VMEM((token_count, width), F32)],
        compiler_params=params(),
    )(pos, back_cold.reshape(GROUPS * NZ * 8, packed), back_hot.reshape(NX * HCAP, wide), back_w)

    swap = [(0, 1), (1, 0)]
    pair = lax.axis_index("pair")
    halves = probs.T.reshape(2, mine, 2)
    own_probs = jnp.where(pair == 0, halves[0], halves[1])
    other_probs = jnp.where(pair == 0, halves[1], halves[0])
    summed = own_rows + lax.ppermute(other_rows, "pair", swap).astype(F32)
    summed_probs = own_probs + lax.ppermute(other_probs, "pair", swap)
    return (summed.astype(BF16), summed_probs, g_gate[None], g_up[None], g_down[None], h_gate, h_up, h_down)


def solution(mesh):
    split = P(("dp", "pair"), None)
    cold = P("dp", "pair", None)
    return jax.shard_map(
        local,
        mesh=mesh,
        in_specs=(P("dp", None),) * 5 + (P(), P()) + (cold,) * 3 + (split,) * 3,
        out_specs=(split, split, cold, cold, cold, split, split, split),
        check_vma=False,
    )
```

```python
import jax
import jax.numpy as jnp
from jax import lax
from jax.experimental import pallas as pl
from jax.experimental.pallas import tpu as pltpu
from jax.sharding import PartitionSpec as P

NX, NY, NZ = 4, 2, 8
CHIPS = NX * NY * NZ
RING = NY * NZ
CAP = 4
HCAP = 48
SIDE = 128
UNIT = 5
GROUPS = NX * NY // 2
MESH = pl.DeviceIdType.MESH
F32 = jnp.float32
BF16 = jnp.bfloat16
VMEM = pltpu.VMEM
ROWS = (((0,), (0,)), ((), ()))
COLS = (((1,), (1,)), ((), ()))


def spec(space):
    return pl.BlockSpec(memory_space=space)


def params(**more):
    return pltpu.CompilerParams(vmem_limit_bytes=56 << 20, **more)


def iota(shape, axis):
    return lax.broadcasted_iota(jnp.int32, shape, axis)


def positions_kernel(flags, owner, ids, slots, out):
    chosen = ids[...]
    count = flags.shape[0]

    def step(entry, carry):
        hot, place = carry
        same = chosen == entry
        hot = jnp.where(same, flags[entry], hot)
        place = jnp.where(same, owner[entry], place)
        return hot, place

    zero = jnp.zeros(chosen.shape, jnp.int32)
    hot, place = lax.fori_loop(0, count, step, (zero, zero))
    slot = slots[...]
    cold_row = jnp.where(slot < CAP, place * CAP + slot, -1)
    hot_row = jnp.where(slot < HCAP, CHIPS * CAP + slot, -1)
    out[...] = jnp.where(hot == 1, hot_row, cold_row)


def cold_match(pos, low, rows, token_count):
    row = low + iota((rows, token_count), 0)
    within = row & 7
    return row, within, (row >> 3) * CAP + (within & 3)


def pack_kernel(flags, owner, ids, slots, probs, tokens, grad, gate, up, down, cold, hot_x, hot_g, weights, pos):
    positions_kernel(flags, owner, ids, slots, pos)
    token_count, width = tokens.shape
    block = 8 * min(CHIPS, 16)
    gates = probs[...].astype(F32)

    def step(index, carry):
        low = pl.multiple_of(index * block, block)
        row, within, want = cold_match(pos, low, block, token_count)
        first = pos[0:1, :] == want
        second = pos[1:2, :] == want
        match = first | second
        pick_x = jnp.where(match & (within < CAP), 1.0, 0.0).astype(BF16)
        pick_g = jnp.where(match & (within >= CAP), 1.0, 0.0).astype(BF16)
        rows = jnp.dot(pick_x, tokens[...], preferred_element_type=F32)
        rows += jnp.dot(pick_g, grad[...], preferred_element_type=F32)
        cold[pl.ds(low, block), :width] = rows.astype(BF16)
        scale = jnp.where(first, gates[0:1, :], 0.0) + jnp.where(second, gates[1:2, :], 0.0)
        scale = jnp.sum(scale, axis=1, keepdims=True)
        cold[pl.ds(low, block), width:] = jnp.broadcast_to(scale, (block, SIDE)).astype(BF16)
        return carry

    lax.fori_loop(0, 8 * CHIPS // block, step, 0)
    want = CHIPS * CAP + iota((HCAP, token_count), 0)
    first = pos[0:1, :] == want
    second = pos[1:2, :] == want
    pick = jnp.where(first | second, 1.0, 0.0).astype(BF16)
    hot_x[:, :width] = jnp.dot(pick, tokens[...], preferred_element_type=F32).astype(BF16)
    hot_g[...] = jnp.dot(pick, grad[...], preferred_element_type=F32).astype(BF16)
    scale = jnp.where(first, gates[0:1, :], 0.0) + jnp.where(second, gates[1:2, :], 0.0)
    hot_x[:, width:] = jnp.broadcast_to(jnp.sum(scale, axis=1, keepdims=True), (HCAP, SIDE)).astype(BF16)
    rest = jnp.zeros((16 - 3 * UNIT, width), F32)
    parts = [gate[...].astype(F32), up[...].astype(F32), down[...].astype(F32), rest]
    weights[...] = jnp.concatenate(parts, axis=0).astype(BF16)


def place():
    me = lax.axis_index("dp")
    core = lax.rem(me, 2)
    chip = lax.div(me, 2)
    ring = lax.rem(chip, RING)
    return lax.axis_index("pair"), core, lax.div(chip, RING), lax.div(ring, NZ), lax.rem(ring, NZ)


def device(x, y, z, core, pair):
    return (((x * NY + y) * NZ + z) * 2 + core, pair)


def remote(src, dst, send, recv, to):
    return pltpu.make_async_remote_copy(
        src_ref=src, dst_ref=dst, send_sem=send, recv_sem=recv, device_id=to, device_id_type=MESH
    )


def swish(pre_gate, pre_up, back, scale):
    sigmoid = 1.0 / (1.0 + jnp.exp(-pre_gate))
    act = pre_gate * sigmoid
    hidden = act * pre_up
    probs = hidden * back
    hidden_grad = scale * back
    gate_grad = hidden_grad * pre_up * sigmoid * (1.0 + pre_gate * (1.0 - sigmoid))
    return gate_grad, hidden_grad * act, scale * hidden, probs


def layer_kernel(
    cold_in, hot_x_in, hot_g_in, w_in, c_gate, c_up, c_down,
    back_cold, back_hot, back_w, cold_out, gate_out, up_out, down_out,
    cold, hot_x, hot_g, w, d_gate, d_up, d_down, d_hot, ret, away, side, pass_on, passed, final,
    hot_ret, hot_away, hot_side, hot_sum, w_ret, w_away, w_side, w_sum,
    own, cold_send, cold_recv, hot_send, hot_recv, w_send, w_recv, near_send, near_recv, over_send, over_recv,
    side_send, side_recv, pass_send, pass_recv, back_send, back_recv, hb_send, hb_recv, wb_send, wb_recv, wy_send, wy_recv, one_send, out_sem,
):
    width = c_gate.shape[1]
    half = width // 2
    pair, core, x, y, z = place()
    sibling = device(x, y, z, 1 - core, pair)
    partner = device(x, y, z, core, 1 - pair)

    def along(kx, ky, kz):
        other_y = lax.rem(y + ky, NY)
        other_pair = lax.rem(pair + ky, 2)
        return device(lax.rem(x + kx, NX), other_y, lax.rem(z + kz, NZ), core, other_pair)

    barrier = pltpu.get_barrier_semaphore()

    def greet(k, carry):
        to = along(lax.div(k, RING), lax.div(lax.rem(k, RING), NZ), lax.rem(k, NZ))
        pl.semaphore_signal(barrier, inc=1, device_id=to, device_id_type=MESH)
        return carry

    lax.fori_loop(1, CHIPS, greet, 0)
    pl.semaphore_signal(barrier, inc=1, device_id=sibling, device_id_type=MESH)
    pl.semaphore_signal(barrier, inc=1, device_id=partner, device_id_type=MESH)
    pl.semaphore_wait(barrier, CHIPS + 1)

    def hot_at(which, k):
        return pl.ds(pl.multiple_of((which * NX + k) * HCAP, HCAP), HCAP)

    mine = [
        pltpu.make_async_copy(hot_x_in, hot_x.at[hot_at(core, 0)], own.at[0]),
        pltpu.make_async_copy(hot_g_in, hot_g.at[hot_at(core, 0)], own.at[1]),
        pltpu.make_async_copy(w_in, w.at[pl.ds(0, 16)], own.at[2]),
    ]
    for copy in mine:
        copy.start()
    for k in range(1, NX):
        remote(hot_x_in, hot_x.at[hot_at(core, k)], hot_send.at[0], hot_recv.at[0], along(k, 0, 0)).start()
        remote(hot_g_in, hot_g.at[hot_at(core, k)], hot_send.at[1], hot_recv.at[1], along(k, 0, 0)).start()

    def send_w(k, carry):
        slot = pl.ds(pl.multiple_of(k * 16, 16), 16)
        remote(w_in, w.at[slot], w_send, w_recv, along(0, 0, k)).start()
        return carry

    lax.fori_loop(1, NZ, send_w, 0)

    def cold_at(group, which):
        return pl.ds((group * 2 + which) * NZ, NZ)

    for j in range(GROUPS):
        kx, ky = pair + 2 * (j // NY), j % NY
        to_x, to_y = lax.rem(x + kx, NX), lax.rem(y + ky, NY)

        def cold_copy(kz, j=j, kx=kx, ky=ky, to_x=to_x, to_y=to_y):
            chip = (to_x * NY + to_y) * NZ + lax.rem(z + kz, NZ)
            slot = (j * 2 + core) * NZ + z
            return cold_in.at[chip], cold.at[slot], along(kx, ky, kz)

        if j == 0:
            src, dst, to = cold_copy(0)

            @pl.when(pair == 0)
            def _():
                pltpu.make_async_copy(src, dst, cold_recv.at[0]).start()

            @pl.when(pair == 1)
            def _():
                remote(src, dst, one_send.at[0], cold_recv.at[0], to).start()

        def send_cold(kz, carry, j=j, cold_copy=cold_copy):
            src, dst, to = cold_copy(kz)
            remote(src, dst, cold_send, cold_recv.at[j], to).start()
            return carry

        lax.fori_loop(1 if j == 0 else 0, NZ, send_cold, 0)

    started = []

    def start(copy):
        copy.start()
        started.append(copy)
        return copy

    mine[0].wait()
    mine[1].wait()
    others = pl.ds(0, (NX - 1) * HCAP)
    remote(hot_x.at[others], hot_x.at[others], hot_send.at[0], hot_recv.at[0], sibling).wait_recv()
    remote(hot_g.at[others], hot_g.at[others], hot_send.at[1], hot_recv.at[1], sibling).wait_recv()
    this = pl.ds(pl.multiple_of(core * NX * HCAP, HCAP), NX * HCAP)
    hot_over = [
        start(remote(hot_x.at[this], hot_x.at[this], over_send.at[2 * GROUPS], over_recv.at[2 * GROUPS], sibling)),
        start(remote(hot_g.at[this], hot_g.at[this], over_send.at[2 * GROUPS + 1], over_recv.at[2 * GROUPS + 1], sibling)),
    ]
    mine[2].wait()
    w_others = pl.ds(0, (NZ - 1) * 16)
    remote(w.at[w_others], w.at[w_others], w_send, w_recv, sibling).wait_recv()
    across = along(0, 1, 0)
    w_here, w_there = pl.ds(0, NZ * 16), pl.ds(NZ * 16, NZ * 16)
    w_over = start(remote(w.at[w_here], w.at[w_there], wy_send.at[0], wy_recv.at[0], across))

    near, over = [], []

    def hand_over(group):
        ref = cold.at[cold_at(group, core)]
        over.append(start(remote(ref, ref, over_send.at[group], over_recv.at[group], sibling)))

    def receive(j):
        ref = cold.at[cold_at(j, core)]
        remote(ref, ref, cold_send, cold_recv.at[j], sibling).wait_recv()
        to = cold.at[cold_at(GROUPS + j, core)]
        near.append(start(remote(ref, to, near_send.at[j], near_recv.at[j], partner)))
        hand_over(j)

    receive(0)
    for copy in hot_over:
        copy.wait_recv()
    w_over.wait_recv()

    units = w.shape[0]
    hot_rows = hot_x.shape[0]
    lane = iota((hot_rows, units), 1) & 15
    scale = hot_x[:, width : width + SIDE].astype(F32)[:, :1]
    pre = lax.dot_general(hot_x[:, :width], w[...], COLS, preferred_element_type=F32)
    project = lax.dot_general(hot_g[...], w[...], COLS, preferred_element_type=F32)
    pre_up = pltpu.roll(pre, units - UNIT, 1)
    project = pltpu.roll(project, units - 2 * UNIT, 1)
    gate_grad, up_grad, weighted, probs = swish(pre, pre_up, project, scale)
    live = lane < UNIT
    up_grad = pltpu.roll(jnp.where(live, up_grad, 0.0), UNIT, 1)
    grads = (jnp.where(live, gate_grad, 0.0) + up_grad).astype(BF16)
    d_hot[:hot_rows, :] = grads
    d_hot[hot_rows:, :] = pltpu.roll(jnp.where(live, weighted, 0.0), 2 * UNIT, 1).astype(BF16)
    hot_ret[:, :width] = jnp.dot(grads, w[...], preferred_element_type=F32)
    probs = jnp.sum(jnp.where(live, probs, 0.0), axis=1, keepdims=True)
    hot_ret[:, width:] = jnp.broadcast_to(probs, (hot_rows, SIDE))
    that = pl.ds(pl.multiple_of((1 - core) * NX * HCAP, HCAP), NX * HCAP)
    hot_away[...] = hot_ret[that, :].astype(BF16)
    hot_swap = start(remote(hot_away, hot_side, side_send.at[2 * GROUPS], side_recv.at[2 * GROUPS], sibling))
    w_grad = lax.dot_general(d_hot[:hot_rows, :], hot_x[:, :width], ROWS, preferred_element_type=F32)
    w_grad += lax.dot_general(d_hot[hot_rows:, :], hot_g[...], ROWS, preferred_element_type=F32)
    w_ret[...] = w_grad[: NZ * 16]
    w_away[...] = w_grad[NZ * 16 :].astype(BF16)
    w_swap = start(remote(w_away, w_side, wy_send.at[1], wy_recv.at[1], across))

    def back(kx, ky, kz):
        return along(lax.rem(NX - kx, NX), ky, NZ - kz)

    for j in range(1, GROUPS):
        receive(j)
    w_swap.wait_recv()
    w_sum[...] = (w_ret[...] + w_side[...].astype(F32)).astype(BF16)

    def return_w(k, carry):
        slot = pl.ds(pl.multiple_of(k * 16, 16), 16)
        remote(w_sum.at[slot], back_w.at[k], wb_send, wb_recv, back(0, 0, k)).start()
        return carry

    lax.fori_loop(1, NZ, return_w, 0)
    mine = [pltpu.make_async_copy(w_sum.at[pl.ds(0, 16)], back_w.at[0], own.at[0])]
    mine[0].start()
    hot_swap.wait_recv()
    for k in range(NX):
        at = pl.ds(k * HCAP, HCAP)
        source = pl.ds(pl.multiple_of((core * NX + k) * HCAP, HCAP), HCAP)
        hot_sum[at, :] = (hot_ret[source, :] + hot_side[at, :].astype(F32)).astype(BF16)
        if k:
            remote(hot_sum.at[at], back_hot.at[k], hb_send, hb_recv, back(k, 0, 0)).start()
        else:
            mine.append(pltpu.make_async_copy(hot_sum.at[at], back_hot.at[0], own.at[1]))
            mine[1].start()
    for j in range(GROUPS):
        near[j].wait_recv()
        hand_over(GROUPS + j)

    block = 4 * 8 * NZ
    side_copies = {}

    def compute(index):
        for group in (2 * index, 2 * index + 1):
            over[group].wait_recv()
        at = slice(index * block, (index + 1) * block)
        data = cold[index * 4 * NZ : (index + 1) * 4 * NZ].reshape(block, width + SIDE)
        scale = data[:, width:].astype(F32)[:, :1]
        data = data[:, :width]
        pre_gate = lax.dot_general(data, c_gate[...], COLS, preferred_element_type=F32)
        pre_up = lax.dot_general(data, c_up[...], COLS, preferred_element_type=F32)
        project = lax.dot_general(data, c_down[...], COLS, preferred_element_type=F32)
        project = pltpu.roll(project, block - CAP, 0)
        gate_grad, up_grad, weighted, probs = swish(pre_gate, pre_up, project, scale)
        is_x = (iota(pre_gate.shape, 0) & 7) < CAP
        gate_grad = jnp.where(is_x, gate_grad, 0.0).astype(BF16)
        up_grad = jnp.where(is_x, up_grad, 0.0).astype(BF16)
        d_gate[at, :] = gate_grad
        d_up[at, :] = up_grad
        d_down[at, :] = pltpu.roll(jnp.where(is_x, weighted, 0.0), CAP, 0).astype(BF16)
        dx = jnp.dot(gate_grad, c_gate[...], preferred_element_type=F32)
        dx += jnp.dot(up_grad, c_up[...], preferred_element_type=F32)
        is_x = (iota((block, half), 0) & 7) < CAP
        ret[at, :half] = jnp.where(is_x, dx[:, :half], pltpu.roll(dx[:, half:], CAP, 0))
        probs = jnp.sum(probs, axis=1, keepdims=True)
        ret[at, half:] = jnp.broadcast_to(probs, (block, SIDE))
        for group in (2 * index, 2 * index + 1):
            away[group] = ret[rows_of(group, 1 - core), :].astype(BF16)
            side_copies[group] = start(remote(away.at[group], side.at[group], side_send.at[group], side_recv.at[group], sibling))

    def rows_of(group, which):
        return pl.ds(pl.multiple_of((group * 2 + which) * 8 * NZ, 8 * NZ), 8 * NZ)

    passes = {}

    def summed(group):
        side_copies[group].wait_recv()
        return ret[rows_of(group, core), :] + side[group].astype(F32)

    def pass_over(j):
        pass_on[j] = summed(GROUPS + j).astype(BF16)
        passes[j] = start(remote(pass_on.at[j], passed.at[j], pass_send.at[j], pass_recv.at[j], partner))

    def give_back(j):
        passes[j].wait_recv()
        value = (summed(j) + passed[j].astype(F32)).astype(BF16)
        final[j * NZ : (j + 1) * NZ] = value.reshape(NZ, 8, half + SIDE)
        ky = j % NY
        kx = lax.rem(pair + ky, 2) + 2 * (j // NY)

        def back_copy(kz):
            source = lax.rem(z + NZ - kz, NZ)
            return final.at[j * NZ + source], back_cold.at[j * NZ + z], back(kx, ky, kz)

        if j == 0:
            src, dst, to = back_copy(0)

            @pl.when(pair == 0)
            def _():
                pltpu.make_async_copy(src, dst, back_recv).start()

            @pl.when(pair == 1)
            def _():
                remote(src, dst, one_send.at[1], back_recv, to).start()

        def send_back(kz, carry):
            src, dst, to = back_copy(kz)
            remote(src, dst, back_send, back_recv, to).start()
            return carry

        lax.fori_loop(1 if j == 0 else 0, NZ, send_back, 0)

    pairs = GROUPS // 2
    for index in range(pairs):
        compute(index)
        if index:
            give_back(2 * index - 2)
            give_back(2 * index - 1)
        compute(pairs + index)
        pass_over(2 * index)
        pass_over(2 * index + 1)
    for k, (source, out) in enumerate(((cold, cold_out), (d_gate, gate_out), (d_up, up_out), (d_down, down_out))):
        mine.append(pltpu.make_async_copy(source, out, out_sem.at[k]))
        mine[-1].start()
    give_back(GROUPS - 2)
    give_back(GROUPS - 1)

    for copy in started:
        copy.wait_send()
    for copy in mine:
        copy.wait()
    for part, send, recv in (
        (hot_x.at[others], hot_send.at[0], None),
        (hot_g.at[others], hot_send.at[1], None),
        (w.at[w_others], w_send, None),
        (cold_in.at[pl.ds(0, GROUPS * NZ - 1)], cold_send, None),
        (final.at[pl.ds(0, GROUPS * NZ - 1)], back_send, None),
        (back_w.at[pl.ds(0, NZ - 1)], wb_send, wb_recv),
        (back_hot.at[pl.ds(0, NX - 1)], hb_send, hb_recv),
    ):
        remote(part, part, send, own.at[0] if recv is None else recv, sibling).wait_send()
        if recv is not None:
            remote(part, part, send, recv, sibling).wait_recv()
    remote(back_cold, back_cold, back_send, back_recv, sibling).wait_recv()

    @pl.when(pair == 1)
    def _():
        remote(cold_in.at[0], cold_in.at[0], one_send.at[0], back_recv, sibling).wait_send()
        remote(final.at[0], final.at[0], one_send.at[1], back_recv, sibling).wait_send()


def unpack_kernel(pos, cold, hot, w, own_rows, other_rows, g_gate, g_up, g_down, total):
    token_count = pos.shape[1]
    half = cold.shape[1] - SIDE
    width = 2 * half
    rows = cold.shape[0]
    mine = token_count // 2
    pair, _, x, y, _ = place()
    row = iota((rows, token_count), 0)
    within = row & 7
    group = lax.div(row, 8 * NZ)
    owner_x = lax.rem(x + pair + 2 * lax.div(group, NY), NX)
    owner_y = lax.rem(y + lax.rem(group, NY), NY)
    owner = (owner_x * NY + owner_y) * NZ + lax.rem(lax.div(row, 8), NZ)
    want = owner * CAP + (within & 3)
    first = pos[0:1, :] == want
    second = pos[1:2, :] == want
    match = first | second

    def pick(mask):
        return jnp.where(mask, 1.0, 0.0).astype(BF16)

    pick_low = pick(match & (within < CAP))
    pick_high = pick(match & (within >= CAP))
    hot_rows = hot.shape[0]
    hot_want = CHIPS * CAP + lax.rem(iota((hot_rows, token_count), 0), HCAP)
    hot_first = pos[0:1, :] == hot_want
    hot_second = pos[1:2, :] == hot_want
    pick_hot = pick(hot_first | hot_second)
    for low, cold_pick in ((0, pick_low), (half, pick_high)):
        part = lax.dot_general(cold_pick, cold[:, :half], ROWS, preferred_element_type=F32)
        part += lax.dot_general(pick_hot, hot[:, low : low + half], ROWS, preferred_element_type=F32)
        total[:, low : low + half] = part
    is_x = within < CAP
    values = []
    for a, b in ((first, hot_first), (second, hot_second)):
        value = lax.dot_general(pick(a & is_x), cold[:, half:], ROWS, preferred_element_type=F32)
        values.append(value + lax.dot_general(pick(b), hot[:, width:], ROWS, preferred_element_type=F32))
    total[:, width:] = jnp.where(iota((token_count, SIDE), 1) == 0, values[0], values[1])
    own_rows[...] = total[pl.ds(pl.multiple_of(pair * mine, 8), mine), :]
    other_rows[...] = total[pl.ds(pl.multiple_of((1 - pair) * mine, 8), mine), :].astype(BF16)
    grads = w[0].astype(F32)
    for k in range(1, w.shape[0]):
        grads += w[k].astype(F32)
    g_gate[...] = grads[0:UNIT].astype(BF16)
    g_up[...] = grads[UNIT : 2 * UNIT].astype(BF16)
    g_down[...] = grads[2 * UNIT : 3 * UNIT].astype(BF16)


def weight_kernel(cold, d_gate, d_up, d_down, g_gate, g_up, g_down):
    width = g_gate.shape[1]
    for grads, out in ((d_gate, g_gate), (d_up, g_up), (d_down, g_down)):
        out[...] = lax.dot_general(grads[...], cold[:, :width], ROWS, preferred_element_type=F32).astype(BF16)


def shape(*dims, dtype=BF16):
    return jax.ShapeDtypeStruct(dims, dtype)


def local(tokens, grad_out, gate_probs, expert_ids, route_slots, hot_flags, owner_slot, cold_gate, cold_up, cold_down, hot_gate, hot_up, hot_down):
    token_count, width = tokens.shape
    wide, half = width + SIDE, width // 2
    ff = cold_gate.shape[1]
    units = 16 * RING
    dma = pltpu.SemaphoreType.DMA
    cold, hot_x, hot_g, weights, pos = pl.pallas_call(
        pack_kernel,
        out_shape=(shape(8 * CHIPS, wide), shape(HCAP, wide), shape(HCAP, width), shape(16, width), shape(2, token_count, dtype=jnp.int32)),
        in_specs=[spec(pltpu.SMEM)] * 2 + [spec(VMEM)] * 8,
        out_specs=[spec(VMEM)] * 5,
        compiler_params=params(),
    )(hot_flags, owner_slot, expert_ids.T, route_slots.T, gate_probs.T, tokens, grad_out, hot_gate, hot_up, hot_down)

    packed = half + SIDE
    lines = 8 * NZ
    hot_rows = 2 * NX * HCAP
    back_cold, back_hot, back_w, rows, d_gate, d_up, d_down = pl.pallas_call(
        layer_kernel,
        out_shape=(shape(GROUPS * NZ, 8, packed), shape(NX, HCAP, wide), shape(NZ, 16, width), shape(2 * CHIPS, 8, wide)) + (shape(16 * CHIPS, ff),) * 3,
        in_specs=[spec(pl.ANY)] * 4 + [spec(VMEM)] * 3,
        out_specs=[spec(pl.ANY)] * 7,
        scratch_shapes=[
            VMEM((2 * CHIPS, 8, wide), BF16), VMEM((hot_rows, wide), BF16), VMEM((hot_rows, width), BF16), VMEM((units, width), BF16),
            VMEM((16 * CHIPS, ff), BF16), VMEM((16 * CHIPS, ff), BF16), VMEM((16 * CHIPS, ff), BF16), VMEM((2 * hot_rows, units), BF16),
            VMEM((16 * CHIPS, packed), F32), VMEM((2 * GROUPS, lines, packed), BF16), VMEM((2 * GROUPS, lines, packed), BF16),
            VMEM((GROUPS, lines, packed), BF16), VMEM((GROUPS, lines, packed), BF16), VMEM((GROUPS * NZ, 8, packed), BF16),
            VMEM((hot_rows, wide), F32), VMEM((NX * HCAP, wide), BF16), VMEM((NX * HCAP, wide), BF16), VMEM((NX * HCAP, wide), BF16), VMEM((NZ * 16, width), F32), VMEM((NZ * 16, width), BF16), VMEM((NZ * 16, width), BF16), VMEM((NZ * 16, width), BF16),
            dma((3,)), dma, dma((GROUPS,)), dma((2,)), dma((2,)), dma, dma, dma((GROUPS,)), dma((GROUPS,)),
            dma((2 * GROUPS + 2,)), dma((2 * GROUPS + 2,)), dma((2 * GROUPS + 1,)), dma((2 * GROUPS + 1,)),
            dma((GROUPS,)), dma((GROUPS,)), dma, dma, dma, dma, dma, dma, dma((2,)), dma((2,)), dma((2,)), dma((4,)),
        ],
        compiler_params=params(collective_id=0, has_side_effects=True),
    )(cold.reshape(CHIPS, 8, wide), hot_x, hot_g, weights, cold_gate[0], cold_up[0], cold_down[0])

    mine = token_count // 2
    own_rows, other_rows, h_gate, h_up, h_down = pl.pallas_call(
        unpack_kernel,
        out_shape=(shape(mine, wide, dtype=F32), shape(mine, wide)) + (shape(UNIT, width),) * 3,
        in_specs=[spec(VMEM)] * 4,
        out_specs=[spec(VMEM)] * 5,
        scratch_shapes=[VMEM((token_count, wide), F32)],
        compiler_params=params(),
    )(pos, back_cold.reshape(GROUPS * NZ * 8, packed), back_hot.reshape(NX * HCAP, wide), back_w)

    swapped = lax.ppermute(other_rows, "pair", [(0, 1), (1, 0)])
    count = 16 * CHIPS
    g_gate, g_up, g_down = pl.pallas_call(
        weight_kernel,
        out_shape=(shape(ff, width),) * 3,
        in_specs=[spec(VMEM)] * 4,
        out_specs=[spec(VMEM)] * 3,
        cost_estimate=pl.CostEstimate(flops=6 * count * ff * width, bytes_accessed=2 * count * (wide + 3 * ff) + 6 * ff * width, transcendentals=0),
        compiler_params=params(),
    )(rows.reshape(count, wide), d_gate, d_up, d_down)
    summed = own_rows + swapped.astype(F32)
    return (summed[:, :width].astype(BF16), summed[:, width : width + 2], g_gate[None], g_up[None], g_down[None], h_gate, h_up, h_down)


def solution(mesh):
    split = P(("dp", "pair"), None)
    cold = P("dp", "pair", None)
    return jax.shard_map(
        local,
        mesh=mesh,
        in_specs=(P("dp", None),) * 5 + (P(), P()) + (cold,) * 3 + (split,) * 3,
        out_specs=(split, split, cold, cold, cold, split, split, split),
        check_vma=False,
    )
```

```python
import jax
import jax.numpy as jnp
from jax import lax
from jax.experimental import pallas as pl
from jax.experimental.pallas import tpu as pltpu
from jax.sharding import PartitionSpec as P

NX, NY, NZ = 4, 2, 8
CHIPS = NX * NY * NZ
RING = NY * NZ
CAP = 4
HCAP = 48
SIDE = 128
UNIT = 5
GROUPS = NX * NY // 2
MESH = pl.DeviceIdType.MESH
F32 = jnp.float32
BF16 = jnp.bfloat16
VMEM = pltpu.VMEM
ROWS = (((0,), (0,)), ((), ()))
COLS = (((1,), (1,)), ((), ()))


def spec(space):
    return pl.BlockSpec(memory_space=space)


def params(**more):
    return pltpu.CompilerParams(vmem_limit_bytes=56 << 20, **more)


def iota(shape, axis):
    return lax.broadcasted_iota(jnp.int32, shape, axis)


def positions_kernel(flags, owner, ids, slots, out):
    chosen = ids[...]
    count = flags.shape[0]

    def step(entry, carry):
        hot, place = carry
        same = chosen == entry
        hot = jnp.where(same, flags[entry], hot)
        place = jnp.where(same, owner[entry], place)
        return hot, place

    zero = jnp.zeros(chosen.shape, jnp.int32)
    hot, place = lax.fori_loop(0, count, step, (zero, zero))
    slot = slots[...]
    cold_row = jnp.where(slot < CAP, place * CAP + slot, -1)
    hot_row = jnp.where(slot < HCAP, CHIPS * CAP + slot, -1)
    out[...] = jnp.where(hot == 1, hot_row, cold_row)


def place():
    me = lax.axis_index("dp")
    core = lax.rem(me, 2)
    chip = lax.div(me, 2)
    ring = lax.rem(chip, RING)
    return lax.axis_index("pair"), core, lax.div(chip, RING), lax.div(ring, NZ), lax.rem(ring, NZ)


def device(x, y, z, core, pair):
    return (((x * NY + y) * NZ + z) * 2 + core, pair)


def remote(src, dst, send, recv, to):
    return pltpu.make_async_remote_copy(
        src_ref=src, dst_ref=dst, send_sem=send, recv_sem=recv, device_id=to, device_id_type=MESH
    )


def swish(pre_gate, pre_up, back, scale):
    sigmoid = 1.0 / (1.0 + jnp.exp(-pre_gate))
    act = pre_gate * sigmoid
    hidden = act * pre_up
    probs = hidden * back
    hidden_grad = scale * back
    gate_grad = hidden_grad * pre_up * sigmoid * (1.0 + pre_gate * (1.0 - sigmoid))
    return gate_grad, hidden_grad * act, scale * hidden, probs


def one_hot(mask):
    return jnp.where(mask, 1.0, 0.0).astype(BF16)


def layer_kernel(
    flags, owner, ids, slots, probs_in, tokens, grad, gate, up, down, c_gate_in, c_up_in, c_down_in,
    pos, back_cold, back_hot, back_w, cold_out, gate_out, up_out, down_out,
    c_gate, c_up, c_down, cold_in, hot_x_in, hot_g_in, w_in, cold, hot_x, hot_g, w, d_gate, d_up, d_down, d_hot, ret, away, side, pass_on, passed, final,
    hot_ret, hot_away, hot_side, hot_sum, w_ret, w_away, w_side, w_sum,
    own, cold_send, cold_recv, hot_send, hot_recv, w_send, w_recv, near_send, near_recv, over_send, over_recv,
    side_send, side_recv, pass_send, pass_recv, back_send, back_recv, hb_send, hb_recv, wb_send, wb_recv, wy_send, wy_recv, one_send, out_sem, load_sem,
):
    token_count, width = tokens.shape
    half = width // 2
    pair, core, x, y, z = place()
    loads = []
    for k, (source, to) in enumerate(((c_gate_in, c_gate), (c_up_in, c_up), (c_down_in, c_down))):
        loads.append(pltpu.make_async_copy(source, to, load_sem.at[k]))
        loads[k].start()
    sibling = device(x, y, z, 1 - core, pair)
    partner = device(x, y, z, core, 1 - pair)

    def along(kx, ky, kz):
        other_y = lax.rem(y + ky, NY)
        other_pair = lax.rem(pair + ky, 2)
        return device(lax.rem(x + kx, NX), other_y, lax.rem(z + kz, NZ), core, other_pair)

    barrier = pltpu.get_barrier_semaphore()

    def greet(k, carry):
        to = along(lax.div(k, RING), lax.div(lax.rem(k, RING), NZ), lax.rem(k, NZ))
        pl.semaphore_signal(barrier, inc=1, device_id=to, device_id_type=MESH)
        return carry

    lax.fori_loop(1, CHIPS, greet, 0)
    pl.semaphore_signal(barrier, inc=1, device_id=sibling, device_id_type=MESH)
    pl.semaphore_signal(barrier, inc=1, device_id=partner, device_id_type=MESH)

    positions_kernel(flags, owner, ids, slots, pos)
    gates = probs_in[...].astype(F32)

    def scale_of(first, second):
        scale = jnp.where(first, gates[0:1, :], 0.0) + jnp.where(second, gates[1:2, :], 0.0)
        return jnp.broadcast_to(jnp.sum(scale, axis=1, keepdims=True), (first.shape[0], SIDE)).astype(BF16)

    want = CHIPS * CAP + iota((HCAP, token_count), 0)
    first, second = pos[0:1, :] == want, pos[1:2, :] == want
    pick = one_hot(first | second)
    hot_x_in[:, :width] = jnp.dot(pick, tokens[...], preferred_element_type=F32).astype(BF16)
    hot_g_in[...] = jnp.dot(pick, grad[...], preferred_element_type=F32).astype(BF16)
    hot_x_in[:, width:] = scale_of(first, second)
    rest = jnp.zeros((16 - 3 * UNIT, width), F32)
    parts = [gate[...].astype(F32), up[...].astype(F32), down[...].astype(F32), rest]
    w_in[...] = jnp.concatenate(parts, axis=0).astype(BF16)

    def pack(j):
        base = (lax.rem(x + pair + 2 * (j // NY), NX) * NY + lax.rem(y + j % NY, NY)) * NZ
        row = iota((8 * NZ, token_count), 0)
        within = row & 7
        want = (base + (row >> 3)) * CAP + (within & 3)
        first, second = pos[0:1, :] == want, pos[1:2, :] == want
        match = first | second
        rows = jnp.dot(one_hot(match & (within < CAP)), tokens[...], preferred_element_type=F32)
        rows += jnp.dot(one_hot(match & (within >= CAP)), grad[...], preferred_element_type=F32)
        at = slice(j * NZ, (j + 1) * NZ)
        cold_in[at, :, :width] = rows.astype(BF16).reshape(NZ, 8, width)
        cold_in[at, :, width:] = scale_of(first, second).reshape(NZ, 8, SIDE)

    for j in range(GROUPS):
        pack(j)
    pl.semaphore_wait(barrier, CHIPS + 1)

    def hot_at(which, k):
        return pl.ds(pl.multiple_of((which * NX + k) * HCAP, HCAP), HCAP)

    mine = [
        pltpu.make_async_copy(hot_x_in, hot_x.at[hot_at(core, 0)], own.at[0]),
        pltpu.make_async_copy(hot_g_in, hot_g.at[hot_at(core, 0)], own.at[1]),
        pltpu.make_async_copy(w_in, w.at[pl.ds(0, 16)], own.at[2]),
    ]
    for copy in mine:
        copy.start()
    for k in range(1, NX):
        remote(hot_x_in, hot_x.at[hot_at(core, k)], hot_send.at[0], hot_recv.at[0], along(k, 0, 0)).start()
        remote(hot_g_in, hot_g.at[hot_at(core, k)], hot_send.at[1], hot_recv.at[1], along(k, 0, 0)).start()

    def send_w(k, carry):
        slot = pl.ds(pl.multiple_of(k * 16, 16), 16)
        remote(w_in, w.at[slot], w_send, w_recv, along(0, 0, k)).start()
        return carry

    lax.fori_loop(1, NZ, send_w, 0)

    def cold_at(group, which):
        return pl.ds((group * 2 + which) * NZ, NZ)

    def issue(j):
        kx, ky = pair + 2 * (j // NY), j % NY

        def cold_copy(kz):
            slot = (j * 2 + core) * NZ + z
            return cold_in.at[j * NZ + lax.rem(z + kz, NZ)], cold.at[slot], along(kx, ky, kz)

        if j == 0:
            src, dst, to = cold_copy(0)

            @pl.when(pair == 0)
            def _():
                pltpu.make_async_copy(src, dst, cold_recv.at[0]).start()

            @pl.when(pair == 1)
            def _():
                remote(src, dst, one_send.at[0], cold_recv.at[0], to).start()

        def send_cold(kz, carry):
            src, dst, to = cold_copy(kz)
            remote(src, dst, cold_send, cold_recv.at[j], to).start()
            return carry

        lax.fori_loop(1 if j == 0 else 0, NZ, send_cold, 0)

    issue(0)
    issue(1)

    started = []

    def start(copy):
        copy.start()
        started.append(copy)
        return copy

    mine[0].wait()
    mine[1].wait()
    others = pl.ds(0, (NX - 1) * HCAP)
    remote(hot_x.at[others], hot_x.at[others], hot_send.at[0], hot_recv.at[0], sibling).wait_recv()
    remote(hot_g.at[others], hot_g.at[others], hot_send.at[1], hot_recv.at[1], sibling).wait_recv()
    this = pl.ds(pl.multiple_of(core * NX * HCAP, HCAP), NX * HCAP)
    hot_over = [
        start(remote(hot_x.at[this], hot_x.at[this], over_send.at[2 * GROUPS], over_recv.at[2 * GROUPS], sibling)),
        start(remote(hot_g.at[this], hot_g.at[this], over_send.at[2 * GROUPS + 1], over_recv.at[2 * GROUPS + 1], sibling)),
    ]
    mine[2].wait()
    w_others = pl.ds(0, (NZ - 1) * 16)
    remote(w.at[w_others], w.at[w_others], w_send, w_recv, sibling).wait_recv()
    across = along(0, 1, 0)
    w_here, w_there = pl.ds(0, NZ * 16), pl.ds(NZ * 16, NZ * 16)
    w_over = start(remote(w.at[w_here], w.at[w_there], wy_send.at[0], wy_recv.at[0], across))

    near, over = [], {}

    def hand_over(group):
        ref = cold.at[cold_at(group, core)]
        over[group] = start(remote(ref, ref, over_send.at[group], over_recv.at[group], sibling))

    def receive(j):
        ref = cold.at[cold_at(j, core)]
        remote(ref, ref, cold_send, cold_recv.at[j], sibling).wait_recv()
        to = cold.at[cold_at(GROUPS + j, core)]
        near.append(start(remote(ref, to, near_send.at[j], near_recv.at[j], partner)))
        hand_over(j)
        if j + 2 < GROUPS:
            issue(j + 2)

    receive(0)
    receive(1)
    for copy in hot_over:
        copy.wait_recv()
    w_over.wait_recv()

    units = w.shape[0]
    hot_rows = hot_x.shape[0]
    lane = iota((hot_rows, units), 1) & 15
    scale = hot_x[:, width : width + SIDE].astype(F32)[:, :1]
    pre = lax.dot_general(hot_x[:, :width], w[...], COLS, preferred_element_type=F32)
    project = lax.dot_general(hot_g[...], w[...], COLS, preferred_element_type=F32)
    pre_up = pltpu.roll(pre, units - UNIT, 1)
    project = pltpu.roll(project, units - 2 * UNIT, 1)
    gate_grad, up_grad, weighted, probs = swish(pre, pre_up, project, scale)
    live = lane < UNIT
    up_grad = pltpu.roll(jnp.where(live, up_grad, 0.0), UNIT, 1)
    grads = (jnp.where(live, gate_grad, 0.0) + up_grad).astype(BF16)
    d_hot[:hot_rows, :] = grads
    d_hot[hot_rows:, :] = pltpu.roll(jnp.where(live, weighted, 0.0), 2 * UNIT, 1).astype(BF16)
    hot_ret[:, :width] = jnp.dot(grads, w[...], preferred_element_type=F32)
    probs = jnp.sum(jnp.where(live, probs, 0.0), axis=1, keepdims=True)
    hot_ret[:, width:] = jnp.broadcast_to(probs, (hot_rows, SIDE))
    that = pl.ds(pl.multiple_of((1 - core) * NX * HCAP, HCAP), NX * HCAP)
    hot_away[...] = hot_ret[that, :].astype(BF16)
    hot_swap = start(remote(hot_away, hot_side, side_send.at[2 * GROUPS], side_recv.at[2 * GROUPS], sibling))
    w_grad = lax.dot_general(d_hot[:hot_rows, :], hot_x[:, :width], ROWS, preferred_element_type=F32)
    w_grad += lax.dot_general(d_hot[hot_rows:, :], hot_g[...], ROWS, preferred_element_type=F32)
    w_ret[...] = w_grad[: NZ * 16]
    w_away[...] = w_grad[NZ * 16 :].astype(BF16)
    w_swap = start(remote(w_away, w_side, wy_send.at[1], wy_recv.at[1], across))

    def back(kx, ky, kz):
        return along(lax.rem(NX - kx, NX), ky, NZ - kz)

    mine = []

    def return_weights():
        w_swap.wait_recv()
        w_sum[...] = (w_ret[...] + w_side[...].astype(F32)).astype(BF16)

        def return_w(k, carry):
            slot = pl.ds(pl.multiple_of(k * 16, 16), 16)
            remote(w_sum.at[slot], back_w.at[k], wb_send, wb_recv, back(0, 0, k)).start()
            return carry

        lax.fori_loop(1, NZ, return_w, 0)
        mine.append(pltpu.make_async_copy(w_sum.at[pl.ds(0, 16)], back_w.at[0], own.at[0]))
        mine[-1].start()
    def return_hot():
        hot_swap.wait_recv()
        for k in range(NX):
            at = pl.ds(k * HCAP, HCAP)
            source = pl.ds(pl.multiple_of((core * NX + k) * HCAP, HCAP), HCAP)
            hot_sum[at, :] = (hot_ret[source, :] + hot_side[at, :].astype(F32)).astype(BF16)
            if k:
                remote(hot_sum.at[at], back_hot.at[k], hb_send, hb_recv, back(k, 0, 0)).start()
            else:
                mine.append(pltpu.make_async_copy(hot_sum.at[at], back_hot.at[0], own.at[1]))
                mine[-1].start()

    def relay(j):
        near[j].wait_recv()
        hand_over(GROUPS + j)

    block = 4 * 8 * NZ
    side_copies = {}

    def compute(index):
        for group in (2 * index, 2 * index + 1):
            over[group].wait_recv()
        at = slice(index * block, (index + 1) * block)
        data = cold[index * 4 * NZ : (index + 1) * 4 * NZ].reshape(block, width + SIDE)
        scale = data[:, width:].astype(F32)[:, :1]
        data = data[:, :width]
        pre_gate = lax.dot_general(data, c_gate[...], COLS, preferred_element_type=F32)
        pre_up = lax.dot_general(data, c_up[...], COLS, preferred_element_type=F32)
        project = lax.dot_general(data, c_down[...], COLS, preferred_element_type=F32)
        project = pltpu.roll(project, block - CAP, 0)
        gate_grad, up_grad, weighted, probs = swish(pre_gate, pre_up, project, scale)
        is_x = (iota(pre_gate.shape, 0) & 7) < CAP
        gate_grad = jnp.where(is_x, gate_grad, 0.0).astype(BF16)
        up_grad = jnp.where(is_x, up_grad, 0.0).astype(BF16)
        d_gate[at, :] = gate_grad
        d_up[at, :] = up_grad
        d_down[at, :] = pltpu.roll(jnp.where(is_x, weighted, 0.0), CAP, 0).astype(BF16)
        dx = jnp.dot(gate_grad, c_gate[...], preferred_element_type=F32)
        dx += jnp.dot(up_grad, c_up[...], preferred_element_type=F32)
        is_x = (iota((block, half), 0) & 7) < CAP
        ret[at, :half] = jnp.where(is_x, dx[:, :half], pltpu.roll(dx[:, half:], CAP, 0))
        probs = jnp.sum(probs, axis=1, keepdims=True)
        ret[at, half:] = jnp.broadcast_to(probs, (block, SIDE))
        for group in (2 * index, 2 * index + 1):
            away[group] = ret[rows_of(group, 1 - core), :].astype(BF16)
            side_copies[group] = start(remote(away.at[group], side.at[group], side_send.at[group], side_recv.at[group], sibling))

    def rows_of(group, which):
        return pl.ds(pl.multiple_of((group * 2 + which) * 8 * NZ, 8 * NZ), 8 * NZ)

    passes = {}

    def summed(group):
        side_copies[group].wait_recv()
        return ret[rows_of(group, core), :] + side[group].astype(F32)

    def pass_over(j):
        pass_on[j] = summed(GROUPS + j).astype(BF16)
        passes[j] = start(remote(pass_on.at[j], passed.at[j], pass_send.at[j], pass_recv.at[j], partner))

    def give_back(j):
        passes[j].wait_recv()
        value = (summed(j) + passed[j].astype(F32)).astype(BF16)
        final[j * NZ : (j + 1) * NZ] = value.reshape(NZ, 8, half + SIDE)
        ky = j % NY
        kx = lax.rem(pair + ky, 2) + 2 * (j // NY)

        def back_copy(kz):
            source = lax.rem(z + NZ - kz, NZ)
            return final.at[j * NZ + source], back_cold.at[j * NZ + z], back(kx, ky, kz)

        if j == 0:
            src, dst, to = back_copy(0)

            @pl.when(pair == 0)
            def _():
                pltpu.make_async_copy(src, dst, back_recv).start()

            @pl.when(pair == 1)
            def _():
                remote(src, dst, one_send.at[1], back_recv, to).start()

        def send_back(kz, carry):
            src, dst, to = back_copy(kz)
            remote(src, dst, back_send, back_recv, to).start()
            return carry

        lax.fori_loop(1 if j == 0 else 0, NZ, send_back, 0)

    def keep(k, source, out):
        mine.append(pltpu.make_async_copy(source, out, out_sem.at[k]))
        mine[-1].start()

    for copy in loads:
        copy.wait()
    relay(0)
    relay(1)
    for j in range(2, GROUPS):
        if j == 2:
            receive(2)
        if j == 3:
            compute(0)
            receive(3)
    if GROUPS == 2:
        compute(0)
    compute(GROUPS // 2)
    return_weights()
    return_hot()
    pass_over(0)
    pass_over(1)
    if GROUPS > 2:
        relay(2)
        compute(1)
        relay(3)
        give_back(0)
        give_back(1)
        compute(3)
        pass_over(2)
        pass_over(3)
    keep(0, cold, cold_out)
    keep(1, d_gate, gate_out)
    keep(2, d_up, up_out)
    keep(3, d_down, down_out)
    give_back(GROUPS - 2)
    give_back(GROUPS - 1)

    for copy in started:
        copy.wait_send()
    for copy in mine:
        copy.wait()
    for part, send, recv in (
        (hot_x.at[others], hot_send.at[0], None),
        (hot_g.at[others], hot_send.at[1], None),
        (w.at[w_others], w_send, None),
        (cold_in.at[pl.ds(0, GROUPS * NZ - 1)], cold_send, None),
        (final.at[pl.ds(0, GROUPS * NZ - 1)], back_send, None),
        (back_w.at[pl.ds(0, NZ - 1)], wb_send, wb_recv),
        (back_hot.at[pl.ds(0, NX - 1)], hb_send, hb_recv),
    ):
        remote(part, part, send, own.at[0] if recv is None else recv, sibling).wait_send()
        if recv is not None:
            remote(part, part, send, recv, sibling).wait_recv()
    remote(back_cold, back_cold, back_send, back_recv, sibling).wait_recv()

    @pl.when(pair == 1)
    def _():
        remote(cold_in.at[0], cold_in.at[0], one_send.at[0], back_recv, sibling).wait_send()
        remote(final.at[0], final.at[0], one_send.at[1], back_recv, sibling).wait_send()


def unpack_kernel(pos, cold, hot, w, own_rows, other_rows, g_gate, g_up, g_down, total):
    token_count = pos.shape[1]
    half = cold.shape[1] - SIDE
    width = 2 * half
    rows = cold.shape[0]
    mine = token_count // 2
    pair, _, x, y, _ = place()
    row = iota((rows, token_count), 0)
    within = row & 7
    group = lax.div(row, 8 * NZ)
    owner_x = lax.rem(x + pair + 2 * lax.div(group, NY), NX)
    owner_y = lax.rem(y + lax.rem(group, NY), NY)
    owner = (owner_x * NY + owner_y) * NZ + lax.rem(lax.div(row, 8), NZ)
    want = owner * CAP + (within & 3)
    first = pos[0:1, :] == want
    second = pos[1:2, :] == want
    match = first | second
    pick_low = one_hot(match & (within < CAP))
    pick_high = one_hot(match & (within >= CAP))
    hot_rows = hot.shape[0]
    hot_want = CHIPS * CAP + lax.rem(iota((hot_rows, token_count), 0), HCAP)
    hot_first = pos[0:1, :] == hot_want
    hot_second = pos[1:2, :] == hot_want
    pick_hot = one_hot(hot_first | hot_second)
    for low, cold_pick in ((0, pick_low), (half, pick_high)):
        part = lax.dot_general(cold_pick, cold[:, :half], ROWS, preferred_element_type=F32)
        part += lax.dot_general(pick_hot, hot[:, low : low + half], ROWS, preferred_element_type=F32)
        total[:, low : low + half] = part
    is_x = within < CAP
    values = []
    for a, b in ((first, hot_first), (second, hot_second)):
        value = lax.dot_general(one_hot(a & is_x), cold[:, half:], ROWS, preferred_element_type=F32)
        values.append(value + lax.dot_general(one_hot(b), hot[:, width:], ROWS, preferred_element_type=F32))
    total[:, width:] = jnp.where(iota((token_count, SIDE), 1) == 0, values[0], values[1])
    own_rows[...] = total[pl.ds(pl.multiple_of(pair * mine, 8), mine), :]
    other_rows[...] = total[pl.ds(pl.multiple_of((1 - pair) * mine, 8), mine), :].astype(BF16)
    grads = w[0].astype(F32)
    for k in range(1, w.shape[0]):
        grads += w[k].astype(F32)
    g_gate[...] = grads[0:UNIT].astype(BF16)
    g_up[...] = grads[UNIT : 2 * UNIT].astype(BF16)
    g_down[...] = grads[2 * UNIT : 3 * UNIT].astype(BF16)


def weight_kernel(cold, d_gate, d_up, d_down, g_gate, g_up, g_down):
    width = g_gate.shape[1]
    for grads, out in ((d_gate, g_gate), (d_up, g_up), (d_down, g_down)):
        out[...] = lax.dot_general(grads[...], cold[:, :width], ROWS, preferred_element_type=F32).astype(BF16)


def shape(*dims, dtype=BF16):
    return jax.ShapeDtypeStruct(dims, dtype)


def local(tokens, grad_out, gate_probs, expert_ids, route_slots, hot_flags, owner_slot, cold_gate, cold_up, cold_down, hot_gate, hot_up, hot_down):
    token_count, width = tokens.shape
    wide, half = width + SIDE, width // 2
    ff = cold_gate.shape[1]
    units = 16 * RING
    dma = pltpu.SemaphoreType.DMA
    packed = half + SIDE
    lines = 8 * NZ
    hot_rows = 2 * NX * HCAP
    pos, back_cold, back_hot, back_w, rows, d_gate, d_up, d_down = pl.pallas_call(
        layer_kernel,
        out_shape=(shape(2, token_count, dtype=jnp.int32), shape(GROUPS * NZ, 8, packed), shape(NX, HCAP, wide), shape(NZ, 16, width), shape(2 * CHIPS, 8, wide)) + (shape(16 * CHIPS, ff),) * 3,
        in_specs=[spec(pltpu.SMEM)] * 2 + [spec(VMEM)] * 8 + [spec(pl.ANY)] * 3,
        out_specs=[spec(VMEM)] + [spec(pl.ANY)] * 7,
        scratch_shapes=[
            VMEM((ff, width), BF16), VMEM((ff, width), BF16), VMEM((ff, width), BF16),
            VMEM((GROUPS * NZ, 8, wide), BF16), VMEM((HCAP, wide), BF16), VMEM((HCAP, width), BF16), VMEM((16, width), BF16),
            VMEM((2 * CHIPS, 8, wide), BF16), VMEM((hot_rows, wide), BF16), VMEM((hot_rows, width), BF16), VMEM((units, width), BF16),
            VMEM((16 * CHIPS, ff), BF16), VMEM((16 * CHIPS, ff), BF16), VMEM((16 * CHIPS, ff), BF16), VMEM((2 * hot_rows, units), BF16),
            VMEM((16 * CHIPS, packed), F32), VMEM((2 * GROUPS, lines, packed), BF16), VMEM((2 * GROUPS, lines, packed), BF16),
            VMEM((GROUPS, lines, packed), BF16), VMEM((GROUPS, lines, packed), BF16), VMEM((GROUPS * NZ, 8, packed), BF16),
            VMEM((hot_rows, wide), F32), VMEM((NX * HCAP, wide), BF16), VMEM((NX * HCAP, wide), BF16), VMEM((NX * HCAP, wide), BF16), VMEM((NZ * 16, width), F32), VMEM((NZ * 16, width), BF16), VMEM((NZ * 16, width), BF16), VMEM((NZ * 16, width), BF16),
            dma((3,)), dma, dma((GROUPS,)), dma((2,)), dma((2,)), dma, dma, dma((GROUPS,)), dma((GROUPS,)),
            dma((2 * GROUPS + 2,)), dma((2 * GROUPS + 2,)), dma((2 * GROUPS + 1,)), dma((2 * GROUPS + 1,)),
            dma((GROUPS,)), dma((GROUPS,)), dma, dma, dma, dma, dma, dma, dma((2,)), dma((2,)), dma((2,)), dma((4,)), dma((3,)),
        ],
        compiler_params=params(collective_id=0, has_side_effects=True),
    )(hot_flags, owner_slot, expert_ids.T, route_slots.T, gate_probs.T, tokens, grad_out, hot_gate, hot_up, hot_down, cold_gate[0], cold_up[0], cold_down[0])

    mine = token_count // 2
    own_rows, other_rows, h_gate, h_up, h_down = pl.pallas_call(
        unpack_kernel,
        out_shape=(shape(mine, wide, dtype=F32), shape(mine, wide)) + (shape(UNIT, width),) * 3,
        in_specs=[spec(VMEM)] * 4,
        out_specs=[spec(VMEM)] * 5,
        scratch_shapes=[VMEM((token_count, wide), F32)],
        compiler_params=params(),
    )(pos, back_cold.reshape(GROUPS * NZ * 8, packed), back_hot.reshape(NX * HCAP, wide), back_w)

    swapped = lax.ppermute(other_rows, "pair", [(0, 1), (1, 0)])
    count = 16 * CHIPS
    g_gate, g_up, g_down = pl.pallas_call(
        weight_kernel,
        out_shape=(shape(ff, width),) * 3,
        in_specs=[spec(VMEM)] * 4,
        out_specs=[spec(VMEM)] * 3,
        cost_estimate=pl.CostEstimate(flops=6 * count * ff * width, bytes_accessed=2 * count * (wide + 3 * ff) + 6 * ff * width, transcendentals=0),
        compiler_params=params(),
    )(rows.reshape(count, wide), d_gate, d_up, d_down)
    summed = own_rows + swapped.astype(F32)
    return (summed[:, :width].astype(BF16), summed[:, width : width + 2], g_gate[None], g_up[None], g_down[None], h_gate, h_up, h_down)


def solution(mesh):
    split = P(("dp", "pair"), None)
    cold = P("dp", "pair", None)
    return jax.shard_map(
        local,
        mesh=mesh,
        in_specs=(P("dp", None),) * 5 + (P(), P()) + (cold,) * 3 + (split,) * 3,
        out_specs=(split, split, cold, cold, cold, split, split, split),
        check_vma=False,
    )
```

```python
import jax
import jax.numpy as jnp
from jax import lax
from jax.experimental import pallas as pl
from jax.experimental.pallas import tpu as pltpu
from jax.sharding import PartitionSpec as P

NX, NY, NZ = 4, 2, 8
CHIPS = NX * NY * NZ
RING = NY * NZ
CAP = 4
HCAP = 48
SIDE = 128
UNIT = 5
GROUPS = NX * NY // 2
MESH = pl.DeviceIdType.MESH
F32 = jnp.float32
BF16 = jnp.bfloat16
VMEM = pltpu.VMEM
ROWS = (((0,), (0,)), ((), ()))
COLS = (((1,), (1,)), ((), ()))


def spec(space):
    return pl.BlockSpec(memory_space=space)


def params(**more):
    return pltpu.CompilerParams(vmem_limit_bytes=56 << 20, **more)


def iota(shape, axis):
    return lax.broadcasted_iota(jnp.int32, shape, axis)


def positions_kernel(flags, owner, ids, slots, out):
    chosen = ids[...]
    count = flags.shape[0]

    def step(entry, carry):
        hot, place = carry
        same = chosen == entry
        hot = jnp.where(same, flags[entry], hot)
        place = jnp.where(same, owner[entry], place)
        return hot, place

    zero = jnp.zeros(chosen.shape, jnp.int32)
    hot, place = lax.fori_loop(0, count, step, (zero, zero))
    slot = slots[...]
    cold_row = jnp.where(slot < CAP, place * CAP + slot, -1)
    hot_row = jnp.where(slot < HCAP, CHIPS * CAP + slot, -1)
    out[...] = jnp.where(hot == 1, hot_row, cold_row)


def place():
    me = lax.axis_index("dp")
    core = lax.rem(me, 2)
    chip = lax.div(me, 2)
    ring = lax.rem(chip, RING)
    return lax.axis_index("pair"), core, lax.div(chip, RING), lax.div(ring, NZ), lax.rem(ring, NZ)


def device(x, y, z, core, pair):
    return (((x * NY + y) * NZ + z) * 2 + core, pair)


def remote(src, dst, send, recv, to):
    return pltpu.make_async_remote_copy(
        src_ref=src, dst_ref=dst, send_sem=send, recv_sem=recv, device_id=to, device_id_type=MESH
    )


def swish(pre_gate, pre_up, back, scale):
    sigmoid = 1.0 / (1.0 + jnp.exp(-pre_gate))
    act = pre_gate * sigmoid
    hidden = act * pre_up
    probs = hidden * back
    hidden_grad = scale * back
    gate_grad = hidden_grad * pre_up * sigmoid * (1.0 + pre_gate * (1.0 - sigmoid))
    return gate_grad, hidden_grad * act, scale * hidden, probs


def one_hot(mask):
    return jnp.where(mask, 1.0, 0.0).astype(BF16)


def layer_kernel(
    flags, owner, ids, slots, probs_in, tokens, grad, gate, up, down, c_gate_in, c_up_in, c_down_in,
    own_rows, other_rows, back_w, cold_out, gate_out, up_out, down_out,
    pos, back_cold, back_hot, total, c_gate, c_up, c_down, cold_in, hot_x_in, hot_g_in, w_in, cold, hot_x, hot_g, w, d_gate, d_up, d_down, d_hot, ret, away, side, pass_on, passed, final,
    hot_ret, hot_away, hot_side, hot_sum, w_ret, w_away, w_side, w_sum,
    own, cold_send, cold_recv, hot_send, hot_recv, w_send, w_recv, near_send, near_recv, over_send, over_recv,
    side_send, side_recv, pass_send, pass_recv, back_send, back_recv, hb_send, hb_recv, wb_send, wb_recv, wy_send, wy_recv, one_send, out_sem, load_sem,
):
    token_count, width = tokens.shape
    half = width // 2
    pair, core, x, y, z = place()
    loads = []
    for k, (source, to) in enumerate(((c_gate_in, c_gate), (c_up_in, c_up), (c_down_in, c_down))):
        loads.append(pltpu.make_async_copy(source, to, load_sem.at[k]))
        loads[k].start()
    sibling = device(x, y, z, 1 - core, pair)
    partner = device(x, y, z, core, 1 - pair)

    def along(kx, ky, kz):
        other_y = lax.rem(y + ky, NY)
        other_pair = lax.rem(pair + ky, 2)
        return device(lax.rem(x + kx, NX), other_y, lax.rem(z + kz, NZ), core, other_pair)

    barrier = pltpu.get_barrier_semaphore()

    def greet(k, carry):
        to = along(lax.div(k, RING), lax.div(lax.rem(k, RING), NZ), lax.rem(k, NZ))
        pl.semaphore_signal(barrier, inc=1, device_id=to, device_id_type=MESH)
        return carry

    lax.fori_loop(1, CHIPS, greet, 0)
    pl.semaphore_signal(barrier, inc=1, device_id=sibling, device_id_type=MESH)
    pl.semaphore_signal(barrier, inc=1, device_id=partner, device_id_type=MESH)

    positions_kernel(flags, owner, ids, slots, pos)
    gates = probs_in[...].astype(F32)

    def scale_of(first, second):
        scale = jnp.where(first, gates[0:1, :], 0.0) + jnp.where(second, gates[1:2, :], 0.0)
        return jnp.broadcast_to(jnp.sum(scale, axis=1, keepdims=True), (first.shape[0], SIDE)).astype(BF16)

    want = CHIPS * CAP + iota((HCAP, token_count), 0)
    first, second = pos[0:1, :] == want, pos[1:2, :] == want
    pick = one_hot(first | second)
    hot_x_in[:, :width] = jnp.dot(pick, tokens[...], preferred_element_type=F32).astype(BF16)
    hot_g_in[...] = jnp.dot(pick, grad[...], preferred_element_type=F32).astype(BF16)
    hot_x_in[:, width:] = scale_of(first, second)
    rest = jnp.zeros((16 - 3 * UNIT, width), F32)
    parts = [gate[...].astype(F32), up[...].astype(F32), down[...].astype(F32), rest]
    w_in[...] = jnp.concatenate(parts, axis=0).astype(BF16)

    def pack():
        row = iota((8 * NZ * GROUPS, token_count), 0)
        within = row & 7
        group = lax.div(row, 8 * NZ)
        to_x = lax.rem(x + pair + 2 * lax.div(group, NY), NX)
        to_y = lax.rem(y + lax.rem(group, NY), NY)
        want = ((to_x * NY + to_y) * NZ + lax.rem(lax.div(row, 8), NZ)) * CAP + (within & 3)
        first, second = pos[0:1, :] == want, pos[1:2, :] == want
        match = first | second
        rows = jnp.dot(one_hot(match & (within < CAP)), tokens[...], preferred_element_type=F32)
        rows += jnp.dot(one_hot(match & (within >= CAP)), grad[...], preferred_element_type=F32)
        cold_in[:, :, :width] = rows.astype(BF16).reshape(GROUPS * NZ, 8, width)
        cold_in[:, :, width:] = scale_of(first, second).reshape(GROUPS * NZ, 8, SIDE)

    pack()
    pl.semaphore_wait(barrier, CHIPS + 1)

    def hot_at(which, k):
        return pl.ds(pl.multiple_of((which * NX + k) * HCAP, HCAP), HCAP)

    mine = [
        pltpu.make_async_copy(hot_x_in, hot_x.at[hot_at(core, 0)], own.at[0]),
        pltpu.make_async_copy(hot_g_in, hot_g.at[hot_at(core, 0)], own.at[1]),
        pltpu.make_async_copy(w_in, w.at[pl.ds(0, 16)], own.at[2]),
    ]
    for copy in mine:
        copy.start()
    for k in range(1, NX):
        remote(hot_x_in, hot_x.at[hot_at(core, k)], hot_send.at[0], hot_recv.at[0], along(k, 0, 0)).start()
        remote(hot_g_in, hot_g.at[hot_at(core, k)], hot_send.at[1], hot_recv.at[1], along(k, 0, 0)).start()

    def send_w(k, carry):
        slot = pl.ds(pl.multiple_of(k * 16, 16), 16)
        remote(w_in, w.at[slot], w_send, w_recv, along(0, 0, k)).start()
        return carry

    lax.fori_loop(1, NZ, send_w, 0)

    def cold_at(group, which):
        return pl.ds((group * 2 + which) * NZ, NZ)

    def issue(j):
        kx, ky = pair + 2 * (j // NY), j % NY

        def cold_copy(kz):
            slot = (j * 2 + core) * NZ + z
            return cold_in.at[j * NZ + lax.rem(z + kz, NZ)], cold.at[slot], along(kx, ky, kz)

        if j == 0:
            src, dst, to = cold_copy(0)

            @pl.when(pair == 0)
            def _():
                pltpu.make_async_copy(src, dst, cold_recv.at[0]).start()

            @pl.when(pair == 1)
            def _():
                remote(src, dst, one_send.at[0], cold_recv.at[0], to).start()

        def send_cold(kz, carry):
            src, dst, to = cold_copy(kz)
            remote(src, dst, cold_send, cold_recv.at[j], to).start()
            return carry

        lax.fori_loop(1 if j == 0 else 0, NZ, send_cold, 0)

    issue(0)
    issue(1)

    started = []

    def start(copy):
        copy.start()
        started.append(copy)
        return copy

    mine[0].wait()
    mine[1].wait()
    others = pl.ds(0, (NX - 1) * HCAP)
    remote(hot_x.at[others], hot_x.at[others], hot_send.at[0], hot_recv.at[0], sibling).wait_recv()
    remote(hot_g.at[others], hot_g.at[others], hot_send.at[1], hot_recv.at[1], sibling).wait_recv()
    this = pl.ds(pl.multiple_of(core * NX * HCAP, HCAP), NX * HCAP)
    hot_over = [
        start(remote(hot_x.at[this], hot_x.at[this], over_send.at[2 * GROUPS], over_recv.at[2 * GROUPS], sibling)),
        start(remote(hot_g.at[this], hot_g.at[this], over_send.at[2 * GROUPS + 1], over_recv.at[2 * GROUPS + 1], sibling)),
    ]
    mine[2].wait()
    w_others = pl.ds(0, (NZ - 1) * 16)
    remote(w.at[w_others], w.at[w_others], w_send, w_recv, sibling).wait_recv()
    across = along(0, 1, 0)
    w_here, w_there = pl.ds(0, NZ * 16), pl.ds(NZ * 16, NZ * 16)
    w_over = start(remote(w.at[w_here], w.at[w_there], wy_send.at[0], wy_recv.at[0], across))

    near, over = [], {}

    def hand_over(group):
        ref = cold.at[cold_at(group, core)]
        over[group] = start(remote(ref, ref, over_send.at[group], over_recv.at[group], sibling))

    def receive(j):
        ref = cold.at[cold_at(j, core)]
        remote(ref, ref, cold_send, cold_recv.at[j], sibling).wait_recv()
        to = cold.at[cold_at(GROUPS + j, core)]
        near.append(start(remote(ref, to, near_send.at[j], near_recv.at[j], partner)))
        hand_over(j)
        if j + 2 < GROUPS:
            issue(j + 2)

    receive(0)
    receive(1)
    for copy in hot_over:
        copy.wait_recv()
    w_over.wait_recv()

    units = w.shape[0]
    hot_rows = hot_x.shape[0]
    lane = iota((hot_rows, units), 1) & 15
    scale = hot_x[:, width : width + SIDE].astype(F32)[:, :1]
    pre = lax.dot_general(hot_x[:, :width], w[...], COLS, preferred_element_type=F32)
    project = lax.dot_general(hot_g[...], w[...], COLS, preferred_element_type=F32)
    pre_up = pltpu.roll(pre, units - UNIT, 1)
    project = pltpu.roll(project, units - 2 * UNIT, 1)
    gate_grad, up_grad, weighted, probs = swish(pre, pre_up, project, scale)
    live = lane < UNIT
    up_grad = pltpu.roll(jnp.where(live, up_grad, 0.0), UNIT, 1)
    grads = (jnp.where(live, gate_grad, 0.0) + up_grad).astype(BF16)
    d_hot[:hot_rows, :] = grads
    d_hot[hot_rows:, :] = pltpu.roll(jnp.where(live, weighted, 0.0), 2 * UNIT, 1).astype(BF16)
    hot_ret[:, :width] = jnp.dot(grads, w[...], preferred_element_type=F32)
    probs = jnp.sum(jnp.where(live, probs, 0.0), axis=1, keepdims=True)
    hot_ret[:, width:] = jnp.broadcast_to(probs, (hot_rows, SIDE))
    that = pl.ds(pl.multiple_of((1 - core) * NX * HCAP, HCAP), NX * HCAP)
    hot_away[...] = hot_ret[that, :].astype(BF16)
    hot_swap = start(remote(hot_away, hot_side, side_send.at[2 * GROUPS], side_recv.at[2 * GROUPS], sibling))
    w_grad = lax.dot_general(d_hot[:hot_rows, :], hot_x[:, :width], ROWS, preferred_element_type=F32)
    w_grad += lax.dot_general(d_hot[hot_rows:, :], hot_g[...], ROWS, preferred_element_type=F32)
    w_ret[...] = w_grad[: NZ * 16]
    w_away[...] = w_grad[NZ * 16 :].astype(BF16)
    w_swap = start(remote(w_away, w_side, wy_send.at[1], wy_recv.at[1], across))

    def back(kx, ky, kz):
        return along(lax.rem(NX - kx, NX), ky, NZ - kz)

    mine = []

    def return_weights():
        w_swap.wait_recv()
        w_sum[...] = (w_ret[...] + w_side[...].astype(F32)).astype(BF16)

        def return_w(k, carry):
            slot = pl.ds(pl.multiple_of(k * 16, 16), 16)
            remote(w_sum.at[slot], back_w.at[k], wb_send, wb_recv, back(0, 0, k)).start()
            return carry

        lax.fori_loop(1, NZ, return_w, 0)
        mine.append(pltpu.make_async_copy(w_sum.at[pl.ds(0, 16)], back_w.at[0], own.at[0]))
        mine[-1].start()
    def return_hot():
        hot_swap.wait_recv()
        for k in range(NX):
            at = pl.ds(k * HCAP, HCAP)
            source = pl.ds(pl.multiple_of((core * NX + k) * HCAP, HCAP), HCAP)
            hot_sum[at, :] = (hot_ret[source, :] + hot_side[at, :].astype(F32)).astype(BF16)
            if k:
                remote(hot_sum.at[at], back_hot.at[k], hb_send, hb_recv, back(k, 0, 0)).start()
            else:
                mine.append(pltpu.make_async_copy(hot_sum.at[at], back_hot.at[0], own.at[1]))
                mine[-1].start()

    def relay(j):
        near[j].wait_recv()
        hand_over(GROUPS + j)

    block = 4 * 8 * NZ
    side_copies = {}

    def compute(index):
        for group in (2 * index, 2 * index + 1):
            over[group].wait_recv()
        at = slice(index * block, (index + 1) * block)
        data = cold[index * 4 * NZ : (index + 1) * 4 * NZ].reshape(block, width + SIDE)
        scale = data[:, width:].astype(F32)[:, :1]
        data = data[:, :width]
        pre_gate = lax.dot_general(data, c_gate[...], COLS, preferred_element_type=F32)
        pre_up = lax.dot_general(data, c_up[...], COLS, preferred_element_type=F32)
        project = lax.dot_general(data, c_down[...], COLS, preferred_element_type=F32)
        project = pltpu.roll(project, block - CAP, 0)
        gate_grad, up_grad, weighted, probs = swish(pre_gate, pre_up, project, scale)
        is_x = (iota(pre_gate.shape, 0) & 7) < CAP
        gate_grad = jnp.where(is_x, gate_grad, 0.0).astype(BF16)
        up_grad = jnp.where(is_x, up_grad, 0.0).astype(BF16)
        d_gate[at, :] = gate_grad
        d_up[at, :] = up_grad
        d_down[at, :] = pltpu.roll(jnp.where(is_x, weighted, 0.0), CAP, 0).astype(BF16)
        dx = jnp.dot(gate_grad, c_gate[...], preferred_element_type=F32)
        dx += jnp.dot(up_grad, c_up[...], preferred_element_type=F32)
        is_x = (iota((block, half), 0) & 7) < CAP
        ret[at, :half] = jnp.where(is_x, dx[:, :half], pltpu.roll(dx[:, half:], CAP, 0))
        probs = jnp.sum(probs, axis=1, keepdims=True)
        ret[at, half:] = jnp.broadcast_to(probs, (block, SIDE))
        for group in (2 * index, 2 * index + 1):
            away[group] = ret[rows_of(group, 1 - core), :].astype(BF16)
            side_copies[group] = start(remote(away.at[group], side.at[group], side_send.at[group], side_recv.at[group], sibling))

    def rows_of(group, which):
        return pl.ds(pl.multiple_of((group * 2 + which) * 8 * NZ, 8 * NZ), 8 * NZ)

    passes = {}

    def summed(group):
        side_copies[group].wait_recv()
        return ret[rows_of(group, core), :] + side[group].astype(F32)

    def pass_over(j):
        pass_on[j] = summed(GROUPS + j).astype(BF16)
        passes[j] = start(remote(pass_on.at[j], passed.at[j], pass_send.at[j], pass_recv.at[j], partner))

    def give_back(j):
        passes[j].wait_recv()
        value = (summed(j) + passed[j].astype(F32)).astype(BF16)
        final[j * NZ : (j + 1) * NZ] = value.reshape(NZ, 8, half + SIDE)
        ky = j % NY
        kx = lax.rem(pair + ky, 2) + 2 * (j // NY)

        def back_copy(kz):
            source = lax.rem(z + NZ - kz, NZ)
            return final.at[j * NZ + source], back_cold.at[j * NZ + z], back(kx, ky, kz)

        if j == 0:
            src, dst, to = back_copy(0)

            @pl.when(pair == 0)
            def _():
                pltpu.make_async_copy(src, dst, back_recv).start()

            @pl.when(pair == 1)
            def _():
                remote(src, dst, one_send.at[1], back_recv, to).start()

        def send_back(kz, carry):
            src, dst, to = back_copy(kz)
            remote(src, dst, back_send, back_recv, to).start()
            return carry

        lax.fori_loop(1 if j == 0 else 0, NZ, send_back, 0)

    def keep(k, source, out):
        mine.append(pltpu.make_async_copy(source, out, out_sem.at[k]))
        mine[-1].start()

    for copy in loads:
        copy.wait()
    relay(0)
    relay(1)
    if GROUPS > 2:
        receive(2)
    compute(0)
    if GROUPS > 2:
        receive(3)
    compute(GROUPS // 2)
    return_weights()
    return_hot()
    pass_over(0)
    pass_over(1)
    if GROUPS > 2:
        relay(2)
        compute(1)
        relay(3)
        give_back(0)
        give_back(1)
        compute(3)
        pass_over(2)
        pass_over(3)
    keep(0, cold, cold_out)
    keep(1, d_gate, gate_out)
    keep(2, d_up, up_out)
    keep(3, d_down, down_out)
    give_back(GROUPS - 2)
    give_back(GROUPS - 1)

    for copy in started:
        copy.wait_send()
    for copy in mine:
        copy.wait()
    for part, send, recv in (
        (hot_x.at[others], hot_send.at[0], None),
        (hot_g.at[others], hot_send.at[1], None),
        (w.at[w_others], w_send, None),
        (cold_in.at[pl.ds(0, GROUPS * NZ - 1)], cold_send, None),
        (final.at[pl.ds(0, GROUPS * NZ - 1)], back_send, None),
        (back_w.at[pl.ds(0, NZ - 1)], wb_send, wb_recv),
        (back_hot.at[pl.ds(0, NX - 1)], hb_send, hb_recv),
    ):
        remote(part, part, send, own.at[0] if recv is None else recv, sibling).wait_send()
        if recv is not None:
            remote(part, part, send, recv, sibling).wait_recv()
    remote(back_cold, back_cold, back_send, back_recv, sibling).wait_recv()

    @pl.when(pair == 1)
    def _():
        remote(cold_in.at[0], cold_in.at[0], one_send.at[0], back_recv, sibling).wait_send()
        remote(final.at[0], final.at[0], one_send.at[1], back_recv, sibling).wait_send()

    rows = 8 * NZ * GROUPS
    returned = back_cold[...].reshape(rows, half + SIDE)
    hot_back = back_hot[...].reshape(NX * HCAP, width + SIDE)
    row = iota((rows, token_count), 0)
    within = row & 7
    group = lax.div(row, 8 * NZ)
    from_x = lax.rem(x + pair + 2 * lax.div(group, NY), NX)
    from_y = lax.rem(y + lax.rem(group, NY), NY)
    chip = (from_x * NY + from_y) * NZ + lax.rem(lax.div(row, 8), NZ)
    want = chip * CAP + (within & 3)
    first = pos[0:1, :] == want
    second = pos[1:2, :] == want
    match = first | second
    pick_low = one_hot(match & (within < CAP))
    pick_high = one_hot(match & (within >= CAP))
    hot_want = CHIPS * CAP + lax.rem(iota((NX * HCAP, token_count), 0), HCAP)
    hot_first = pos[0:1, :] == hot_want
    hot_second = pos[1:2, :] == hot_want
    pick_hot = one_hot(hot_first | hot_second)
    for low, cold_pick in ((0, pick_low), (half, pick_high)):
        part = lax.dot_general(cold_pick, returned[:, :half], ROWS, preferred_element_type=F32)
        part += lax.dot_general(pick_hot, hot_back[:, low : low + half], ROWS, preferred_element_type=F32)
        total[:, low : low + half] = part
    is_x = within < CAP
    values = []
    for a, b in ((first, hot_first), (second, hot_second)):
        value = lax.dot_general(one_hot(a & is_x), returned[:, half:], ROWS, preferred_element_type=F32)
        values.append(value + lax.dot_general(one_hot(b), hot_back[:, width:], ROWS, preferred_element_type=F32))
    total[:, width:] = jnp.where(iota((token_count, SIDE), 1) == 0, values[0], values[1])
    count = token_count // 2
    own_rows[...] = total[pl.ds(pl.multiple_of(pair * count, 16), count), :]
    other_rows[...] = total[pl.ds(pl.multiple_of((1 - pair) * count, 16), count), :].astype(BF16)


def weight_kernel(cold, d_gate, d_up, d_down, w, g_gate, g_up, g_down, h_gate, h_up, h_down):
    width = g_gate.shape[1]
    for grads, out in ((d_gate, g_gate), (d_up, g_up), (d_down, g_down)):
        out[...] = lax.dot_general(grads[...], cold[:, :width], ROWS, preferred_element_type=F32).astype(BF16)
    sums = w[0].astype(F32)
    for k in range(1, w.shape[0]):
        sums += w[k].astype(F32)
    h_gate[...] = sums[0:UNIT].astype(BF16)
    h_up[...] = sums[UNIT : 2 * UNIT].astype(BF16)
    h_down[...] = sums[2 * UNIT : 3 * UNIT].astype(BF16)


def shape(*dims, dtype=BF16):
    return jax.ShapeDtypeStruct(dims, dtype)


def local(tokens, grad_out, gate_probs, expert_ids, route_slots, hot_flags, owner_slot, cold_gate, cold_up, cold_down, hot_gate, hot_up, hot_down):
    token_count, width = tokens.shape
    wide, half = width + SIDE, width // 2
    ff = cold_gate.shape[1]
    units = 16 * RING
    dma = pltpu.SemaphoreType.DMA
    packed = half + SIDE
    lines = 8 * NZ
    hot_rows = 2 * NX * HCAP
    own_rows, other_rows, back_w, rows, d_gate, d_up, d_down = pl.pallas_call(
        layer_kernel,
        out_shape=(shape(token_count // 2, wide, dtype=F32), shape(token_count // 2, wide), shape(NZ, 16, width), shape(2 * CHIPS, 8, wide)) + (shape(16 * CHIPS, ff),) * 3,
        in_specs=[spec(pltpu.SMEM)] * 2 + [spec(VMEM)] * 8 + [spec(pl.ANY)] * 3,
        out_specs=[spec(VMEM)] * 2 + [spec(pl.ANY)] * 5,
        scratch_shapes=[
            VMEM((2, token_count), jnp.int32), VMEM((GROUPS * NZ, 8, packed), BF16), VMEM((NX, HCAP, wide), BF16), VMEM((token_count, wide), F32),
            VMEM((ff, width), BF16), VMEM((ff, width), BF16), VMEM((ff, width), BF16),
            VMEM((GROUPS * NZ, 8, wide), BF16), VMEM((HCAP, wide), BF16), VMEM((HCAP, width), BF16), VMEM((16, width), BF16),
            VMEM((2 * CHIPS, 8, wide), BF16), VMEM((hot_rows, wide), BF16), VMEM((hot_rows, width), BF16), VMEM((units, width), BF16),
            VMEM((16 * CHIPS, ff), BF16), VMEM((16 * CHIPS, ff), BF16), VMEM((16 * CHIPS, ff), BF16), VMEM((2 * hot_rows, units), BF16),
            VMEM((16 * CHIPS, packed), F32), VMEM((2 * GROUPS, lines, packed), BF16), VMEM((2 * GROUPS, lines, packed), BF16),
            VMEM((GROUPS, lines, packed), BF16), VMEM((GROUPS, lines, packed), BF16), VMEM((GROUPS * NZ, 8, packed), BF16),
            VMEM((hot_rows, wide), F32), VMEM((NX * HCAP, wide), BF16), VMEM((NX * HCAP, wide), BF16), VMEM((NX * HCAP, wide), BF16), VMEM((NZ * 16, width), F32), VMEM((NZ * 16, width), BF16), VMEM((NZ * 16, width), BF16), VMEM((NZ * 16, width), BF16),
            dma((3,)), dma, dma((GROUPS,)), dma((2,)), dma((2,)), dma, dma, dma((GROUPS,)), dma((GROUPS,)),
            dma((2 * GROUPS + 2,)), dma((2 * GROUPS + 2,)), dma((2 * GROUPS + 1,)), dma((2 * GROUPS + 1,)),
            dma((GROUPS,)), dma((GROUPS,)), dma, dma, dma, dma, dma, dma, dma((2,)), dma((2,)), dma((2,)), dma((4,)), dma((3,)),
        ],
        compiler_params=params(collective_id=0, has_side_effects=True),
    )(hot_flags, owner_slot, expert_ids.T, route_slots.T, gate_probs.T, tokens, grad_out, hot_gate, hot_up, hot_down, cold_gate[0], cold_up[0], cold_down[0])

    swapped = lax.ppermute(other_rows, "pair", [(0, 1), (1, 0)])
    count = 16 * CHIPS
    g_gate, g_up, g_down, h_gate, h_up, h_down = pl.pallas_call(
        weight_kernel,
        out_shape=(shape(ff, width),) * 3 + (shape(UNIT, width),) * 3,
        in_specs=[spec(VMEM)] * 5,
        out_specs=[spec(VMEM)] * 6,
        cost_estimate=pl.CostEstimate(flops=6 * count * ff * width, bytes_accessed=2 * count * (wide + 3 * ff) + 6 * ff * width, transcendentals=0),
        compiler_params=params(),
    )(rows.reshape(count, wide), d_gate, d_up, d_down, back_w)
    summed = own_rows + swapped.astype(F32)
    return (summed[:, :width].astype(BF16), summed[:, width : width + 2], g_gate[None], g_up[None], g_down[None], h_gate, h_up, h_down)


def solution(mesh):
    split = P(("dp", "pair"), None)
    cold = P("dp", "pair", None)
    return jax.shard_map(
        local,
        mesh=mesh,
        in_specs=(P("dp", None),) * 5 + (P(), P()) + (cold,) * 3 + (split,) * 3,
        out_specs=(split, split, cold, cold, cold, split, split, split),
        check_vma=False,
    )
```

```python
import jax
import jax.numpy as jnp
from jax import lax
from jax.experimental import pallas as pl
from jax.experimental.pallas import tpu as pltpu
from jax.sharding import PartitionSpec as P

NX, NY, NZ = 4, 2, 8
CHIPS = NX * NY * NZ
RING = NY * NZ
CAP = 4
HCAP = 48
SIDE = 128
UNIT = 5
GROUPS = NX * NY // 2
MESH = pl.DeviceIdType.MESH
F32 = jnp.float32
BF16 = jnp.bfloat16
VMEM = pltpu.VMEM
ROWS = (((0,), (0,)), ((), ()))
COLS = (((1,), (1,)), ((), ()))


def spec(space):
    return pl.BlockSpec(memory_space=space)


def params(**more):
    return pltpu.CompilerParams(vmem_limit_bytes=56 << 20, **more)


def iota(shape, axis):
    return lax.broadcasted_iota(jnp.int32, shape, axis)


def positions_kernel(flags, owner, ids, slots, out):
    chosen = ids[...]
    count = flags.shape[0]

    def step(entry, carry):
        hot, place = carry
        same = chosen == entry
        hot = jnp.where(same, flags[entry], hot)
        place = jnp.where(same, owner[entry], place)
        return hot, place

    zero = jnp.zeros(chosen.shape, jnp.int32)
    hot, place = lax.fori_loop(0, count, step, (zero, zero))
    slot = slots[...]
    cold_row = jnp.where(slot < CAP, place * CAP + slot, -1)
    hot_row = jnp.where(slot < HCAP, CHIPS * CAP + slot, -1)
    out[...] = jnp.where(hot == 1, hot_row, cold_row)


def place():
    me = lax.axis_index("dp")
    core = lax.rem(me, 2)
    chip = lax.div(me, 2)
    ring = lax.rem(chip, RING)
    return lax.axis_index("pair"), core, lax.div(chip, RING), lax.div(ring, NZ), lax.rem(ring, NZ)


def device(x, y, z, core, pair):
    return (((x * NY + y) * NZ + z) * 2 + core, pair)


def remote(src, dst, send, recv, to):
    return pltpu.make_async_remote_copy(
        src_ref=src, dst_ref=dst, send_sem=send, recv_sem=recv, device_id=to, device_id_type=MESH
    )


def swish(pre_gate, pre_up, back, scale):
    sigmoid = 1.0 / (1.0 + jnp.exp(-pre_gate))
    act = pre_gate * sigmoid
    hidden = act * pre_up
    probs = hidden * back
    hidden_grad = scale * back
    gate_grad = hidden_grad * pre_up * sigmoid * (1.0 + pre_gate * (1.0 - sigmoid))
    return gate_grad, hidden_grad * act, scale * hidden, probs


def one_hot(mask):
    return jnp.where(mask, 1.0, 0.0).astype(BF16)


def layer_kernel(
    flags, owner, ids, slots, probs_in, tokens, grad, gate, up, down, c_gate_in, c_up_in, c_down_in,
    own_rows, other_rows, back_w, cold_out, gate_out, up_out, down_out,
    pos, back_cold, back_hot, total, c_gate, c_up, c_down, cold_in, hot_x_in, hot_g_in, w_in, cold, hot_x, hot_g, w, d_gate, d_up, d_down, d_hot, ret, away, side, pass_on, passed, final,
    hot_ret, hot_away, hot_side, hot_sum, w_ret, w_away, w_side, w_sum,
    own, cold_send, cold_recv, hot_send, hot_recv, w_send, w_recv, near_send, near_recv, over_send, over_recv,
    side_send, side_recv, pass_send, pass_recv, back_send, back_recv, hb_send, hb_recv, wb_send, wb_recv, wy_send, wy_recv, one_send, out_sem, load_sem,
):
    token_count, width = tokens.shape
    half = width // 2
    pair, core, x, y, z = place()
    loads = []
    for k, (source, to) in enumerate(((c_gate_in, c_gate), (c_up_in, c_up), (c_down_in, c_down))):
        loads.append(pltpu.make_async_copy(source, to, load_sem.at[k]))
        loads[k].start()
    sibling = device(x, y, z, 1 - core, pair)
    partner = device(x, y, z, core, 1 - pair)

    def along(kx, ky, kz):
        other_y = lax.rem(y + ky, NY)
        other_pair = lax.rem(pair + ky, 2)
        return device(lax.rem(x + kx, NX), other_y, lax.rem(z + kz, NZ), core, other_pair)

    barrier = pltpu.get_barrier_semaphore()

    def greet(k, carry):
        to = along(lax.div(k, RING), lax.div(lax.rem(k, RING), NZ), lax.rem(k, NZ))
        pl.semaphore_signal(barrier, inc=1, device_id=to, device_id_type=MESH)
        return carry

    lax.fori_loop(1, CHIPS, greet, 0)
    pl.semaphore_signal(barrier, inc=1, device_id=sibling, device_id_type=MESH)
    pl.semaphore_signal(barrier, inc=1, device_id=partner, device_id_type=MESH)

    positions_kernel(flags, owner, ids, slots, pos)
    gates = probs_in[...].astype(F32)

    def scale_of(first, second):
        scale = jnp.where(first, gates[0:1, :], 0.0) + jnp.where(second, gates[1:2, :], 0.0)
        return jnp.broadcast_to(jnp.sum(scale, axis=1, keepdims=True), (first.shape[0], SIDE)).astype(BF16)

    want = CHIPS * CAP + iota((HCAP, token_count), 0)
    first, second = pos[0:1, :] == want, pos[1:2, :] == want
    pick = one_hot(first | second)
    hot_x_in[:, :width] = jnp.dot(pick, tokens[...], preferred_element_type=F32).astype(BF16)
    hot_g_in[...] = jnp.dot(pick, grad[...], preferred_element_type=F32).astype(BF16)
    hot_x_in[:, width:] = scale_of(first, second)
    rest = jnp.zeros((16 - 3 * UNIT, width), F32)
    parts = [gate[...].astype(F32), up[...].astype(F32), down[...].astype(F32), rest]
    w_in[...] = jnp.concatenate(parts, axis=0).astype(BF16)

    def pack():
        row = iota((8 * NZ * GROUPS, token_count), 0)
        within = row & 7
        group = lax.div(row, 8 * NZ)
        to_x = lax.rem(x + pair + 2 * lax.div(group, NY), NX)
        to_y = lax.rem(y + lax.rem(group, NY), NY)
        want = ((to_x * NY + to_y) * NZ + lax.rem(lax.div(row, 8), NZ)) * CAP + (within & 3)
        first, second = pos[0:1, :] == want, pos[1:2, :] == want
        match = first | second
        rows = jnp.dot(one_hot(match & (within < CAP)), tokens[...], preferred_element_type=F32)
        rows += jnp.dot(one_hot(match & (within >= CAP)), grad[...], preferred_element_type=F32)
        cold_in[:, :, :width] = rows.astype(BF16).reshape(GROUPS * NZ, 8, width)
        cold_in[:, :, width:] = scale_of(first, second).reshape(GROUPS * NZ, 8, SIDE)

    pack()
    pl.semaphore_wait(barrier, CHIPS + 1)

    def hot_at(which, k):
        return pl.ds(pl.multiple_of((which * NX + k) * HCAP, HCAP), HCAP)

    mine = [
        pltpu.make_async_copy(hot_x_in, hot_x.at[hot_at(core, 0)], own.at[0]),
        pltpu.make_async_copy(hot_g_in, hot_g.at[hot_at(core, 0)], own.at[1]),
        pltpu.make_async_copy(w_in, w.at[pl.ds(0, 16)], own.at[2]),
    ]
    for copy in mine:
        copy.start()
    for k in range(1, NX):
        remote(hot_x_in, hot_x.at[hot_at(core, k)], hot_send.at[0], hot_recv.at[0], along(k, 0, 0)).start()
        remote(hot_g_in, hot_g.at[hot_at(core, k)], hot_send.at[1], hot_recv.at[1], along(k, 0, 0)).start()

    def send_w(k, carry):
        slot = pl.ds(pl.multiple_of(k * 16, 16), 16)
        remote(w_in, w.at[slot], w_send, w_recv, along(0, 0, k)).start()
        return carry

    lax.fori_loop(1, NZ, send_w, 0)

    def cold_at(group, which):
        return pl.ds((group * 2 + which) * NZ, NZ)

    def issue(j):
        kx, ky = pair + 2 * (j // NY), j % NY

        def cold_copy(kz):
            slot = (j * 2 + core) * NZ + z
            return cold_in.at[j * NZ + lax.rem(z + kz, NZ)], cold.at[slot], along(kx, ky, kz)

        if j == 0:
            src, dst, to = cold_copy(0)

            @pl.when(pair == 0)
            def _():
                pltpu.make_async_copy(src, dst, cold_recv.at[0]).start()

            @pl.when(pair == 1)
            def _():
                remote(src, dst, one_send.at[0], cold_recv.at[0], to).start()

        def send_cold(kz, carry):
            src, dst, to = cold_copy(kz)
            remote(src, dst, cold_send, cold_recv.at[j], to).start()
            return carry

        lax.fori_loop(1 if j == 0 else 0, NZ, send_cold, 0)

    issue(0)
    issue(1)

    started = []

    def start(copy):
        copy.start()
        started.append(copy)
        return copy

    mine[0].wait()
    mine[1].wait()
    others = pl.ds(0, (NX - 1) * HCAP)
    remote(hot_x.at[others], hot_x.at[others], hot_send.at[0], hot_recv.at[0], sibling).wait_recv()
    remote(hot_g.at[others], hot_g.at[others], hot_send.at[1], hot_recv.at[1], sibling).wait_recv()
    this = pl.ds(pl.multiple_of(core * NX * HCAP, HCAP), NX * HCAP)
    hot_over = [
        start(remote(hot_x.at[this], hot_x.at[this], over_send.at[2 * GROUPS], over_recv.at[2 * GROUPS], sibling)),
        start(remote(hot_g.at[this], hot_g.at[this], over_send.at[2 * GROUPS + 1], over_recv.at[2 * GROUPS + 1], sibling)),
    ]
    mine[2].wait()
    w_others = pl.ds(0, (NZ - 1) * 16)
    remote(w.at[w_others], w.at[w_others], w_send, w_recv, sibling).wait_recv()
    across = along(0, 1, 0)
    w_here, w_there = pl.ds(0, NZ * 16), pl.ds(NZ * 16, NZ * 16)
    w_over = start(remote(w.at[w_here], w.at[w_there], wy_send.at[0], wy_recv.at[0], across))

    near, over = [], {}

    def hand_over(group):
        ref = cold.at[cold_at(group, core)]
        over[group] = start(remote(ref, ref, over_send.at[group], over_recv.at[group], sibling))

    def receive(j):
        ref = cold.at[cold_at(j, core)]
        remote(ref, ref, cold_send, cold_recv.at[j], sibling).wait_recv()
        to = cold.at[cold_at(GROUPS + j, core)]
        near.append(start(remote(ref, to, near_send.at[j], near_recv.at[j], partner)))
        hand_over(j)
        if j + 2 < GROUPS:
            issue(j + 2)

    receive(0)
    receive(1)
    for copy in hot_over:
        copy.wait_recv()
    w_over.wait_recv()

    units = w.shape[0]
    hot_rows = hot_x.shape[0]
    lane = iota((hot_rows, units), 1) & 15
    scale = hot_x[:, width : width + SIDE].astype(F32)[:, :1]
    pre = lax.dot_general(hot_x[:, :width], w[...], COLS, preferred_element_type=F32)
    project = lax.dot_general(hot_g[...], w[...], COLS, preferred_element_type=F32)
    pre_up = pltpu.roll(pre, units - UNIT, 1)
    project = pltpu.roll(project, units - 2 * UNIT, 1)
    gate_grad, up_grad, weighted, probs = swish(pre, pre_up, project, scale)
    live = lane < UNIT
    up_grad = pltpu.roll(jnp.where(live, up_grad, 0.0), UNIT, 1)
    grads = (jnp.where(live, gate_grad, 0.0) + up_grad).astype(BF16)
    d_hot[:hot_rows, :] = grads
    d_hot[hot_rows:, :] = pltpu.roll(jnp.where(live, weighted, 0.0), 2 * UNIT, 1).astype(BF16)
    hot_ret[:, :width] = jnp.dot(grads, w[...], preferred_element_type=F32)
    probs = jnp.sum(jnp.where(live, probs, 0.0), axis=1, keepdims=True)
    hot_ret[:, width:] = jnp.broadcast_to(probs, (hot_rows, SIDE))
    that = pl.ds(pl.multiple_of((1 - core) * NX * HCAP, HCAP), NX * HCAP)
    hot_away[...] = hot_ret[that, :].astype(BF16)
    hot_swap = start(remote(hot_away, hot_side, side_send.at[2 * GROUPS], side_recv.at[2 * GROUPS], sibling))
    w_grad = lax.dot_general(d_hot[:hot_rows, :], hot_x[:, :width], ROWS, preferred_element_type=F32)
    w_grad += lax.dot_general(d_hot[hot_rows:, :], hot_g[...], ROWS, preferred_element_type=F32)
    w_ret[...] = w_grad[: NZ * 16]
    w_away[...] = w_grad[NZ * 16 :].astype(BF16)
    w_swap = start(remote(w_away, w_side, wy_send.at[1], wy_recv.at[1], across))

    def back(kx, ky, kz):
        return along(lax.rem(NX - kx, NX), ky, NZ - kz)

    mine = []

    def return_weights():
        w_swap.wait_recv()
        w_sum[...] = (w_ret[...] + w_side[...].astype(F32)).astype(BF16)

        def return_w(k, carry):
            slot = pl.ds(pl.multiple_of(k * 16, 16), 16)
            remote(w_sum.at[slot], back_w.at[k], wb_send, wb_recv, back(0, 0, k)).start()
            return carry

        lax.fori_loop(1, NZ, return_w, 0)
        mine.append(pltpu.make_async_copy(w_sum.at[pl.ds(0, 16)], back_w.at[0], own.at[0]))
        mine[-1].start()
    def return_hot():
        hot_swap.wait_recv()
        for k in range(NX):
            at = pl.ds(k * HCAP, HCAP)
            source = pl.ds(pl.multiple_of((core * NX + k) * HCAP, HCAP), HCAP)
            hot_sum[at, :] = (hot_ret[source, :] + hot_side[at, :].astype(F32)).astype(BF16)
            if k:
                remote(hot_sum.at[at], back_hot.at[k], hb_send, hb_recv, back(k, 0, 0)).start()
            else:
                mine.append(pltpu.make_async_copy(hot_sum.at[at], back_hot.at[0], own.at[1]))
                mine[-1].start()

    def relay(j):
        near[j].wait_recv()
        hand_over(GROUPS + j)

    block = 4 * 8 * NZ
    side_copies = {}

    def compute(index):
        for group in (2 * index, 2 * index + 1):
            over[group].wait_recv()
        at = slice(index * block, (index + 1) * block)
        data = cold[index * 4 * NZ : (index + 1) * 4 * NZ].reshape(block, width + SIDE)
        scale = data[:, width:].astype(F32)[:, :1]
        data = data[:, :width]
        pre_gate = lax.dot_general(data, c_gate[...], COLS, preferred_element_type=F32)
        pre_up = lax.dot_general(data, c_up[...], COLS, preferred_element_type=F32)
        project = lax.dot_general(data, c_down[...], COLS, preferred_element_type=F32)
        project = pltpu.roll(project, block - CAP, 0)
        gate_grad, up_grad, weighted, probs = swish(pre_gate, pre_up, project, scale)
        is_x = (iota(pre_gate.shape, 0) & 7) < CAP
        gate_grad = jnp.where(is_x, gate_grad, 0.0).astype(BF16)
        up_grad = jnp.where(is_x, up_grad, 0.0).astype(BF16)
        d_gate[at, :] = gate_grad
        d_up[at, :] = up_grad
        d_down[at, :] = pltpu.roll(jnp.where(is_x, weighted, 0.0), CAP, 0).astype(BF16)
        dx = jnp.dot(gate_grad, c_gate[...], preferred_element_type=F32)
        dx += jnp.dot(up_grad, c_up[...], preferred_element_type=F32)
        is_x = (iota((block, half), 0) & 7) < CAP
        ret[at, :half] = jnp.where(is_x, dx[:, :half], pltpu.roll(dx[:, half:], CAP, 0))
        probs = jnp.sum(probs, axis=1, keepdims=True)
        ret[at, half:] = jnp.broadcast_to(probs, (block, SIDE))
        for group in (2 * index, 2 * index + 1):
            away[group] = ret[rows_of(group, 1 - core), :].astype(BF16)
            side_copies[group] = start(remote(away.at[group], side.at[group], side_send.at[group], side_recv.at[group], sibling))

    def rows_of(group, which):
        return pl.ds(pl.multiple_of((group * 2 + which) * 8 * NZ, 8 * NZ), 8 * NZ)

    passes = {}

    def summed(group):
        side_copies[group].wait_recv()
        return ret[rows_of(group, core), :] + side[group].astype(F32)

    def pass_over(j):
        pass_on[j] = summed(GROUPS + j).astype(BF16)
        passes[j] = start(remote(pass_on.at[j], passed.at[j], pass_send.at[j], pass_recv.at[j], partner))

    def give_back(j):
        passes[j].wait_recv()
        value = (summed(j) + passed[j].astype(F32)).astype(BF16)
        final[j * NZ : (j + 1) * NZ] = value.reshape(NZ, 8, half + SIDE)
        ky = j % NY
        kx = lax.rem(pair + ky, 2) + 2 * (j // NY)

        def back_copy(kz):
            source = lax.rem(z + NZ - kz, NZ)
            return final.at[j * NZ + source], back_cold.at[j * NZ + z], back(kx, ky, kz)

        if j == 0:
            src, dst, to = back_copy(0)

            @pl.when(pair == 0)
            def _():
                pltpu.make_async_copy(src, dst, back_recv).start()

            @pl.when(pair == 1)
            def _():
                remote(src, dst, one_send.at[1], back_recv, to).start()

        def send_back(kz, carry):
            src, dst, to = back_copy(kz)
            remote(src, dst, back_send, back_recv, to).start()
            return carry

        lax.fori_loop(1 if j == 0 else 0, NZ, send_back, 0)

    def keep(k, source, out):
        mine.append(pltpu.make_async_copy(source, out, out_sem.at[k]))
        mine[-1].start()

    for copy in loads:
        copy.wait()
    relay(0)
    relay(1)
    if GROUPS > 2:
        receive(2)
    compute(0)
    if GROUPS > 2:
        receive(3)
    compute(GROUPS // 2)
    if GROUPS == 2:
        return_weights()
        return_hot()
    pass_over(0)
    pass_over(1)
    if GROUPS > 2:
        relay(2)
        return_weights()
        compute(1)
        relay(3)
        return_hot()
        give_back(0)
        give_back(1)
        compute(3)
        pass_over(2)
        pass_over(3)
    keep(0, cold, cold_out)
    keep(1, d_gate, gate_out)
    keep(2, d_up, up_out)
    keep(3, d_down, down_out)
    give_back(GROUPS - 2)
    give_back(GROUPS - 1)

    for copy in started:
        copy.wait_send()
    for copy in mine:
        copy.wait()
    for part, send, recv in (
        (hot_x.at[others], hot_send.at[0], None),
        (hot_g.at[others], hot_send.at[1], None),
        (w.at[w_others], w_send, None),
        (cold_in.at[pl.ds(0, GROUPS * NZ - 1)], cold_send, None),
        (final.at[pl.ds(0, GROUPS * NZ - 1)], back_send, None),
        (back_w.at[pl.ds(0, NZ - 1)], wb_send, wb_recv),
        (back_hot.at[pl.ds(0, NX - 1)], hb_send, hb_recv),
    ):
        remote(part, part, send, own.at[0] if recv is None else recv, sibling).wait_send()
        if recv is not None:
            remote(part, part, send, recv, sibling).wait_recv()
    remote(back_cold, back_cold, back_send, back_recv, sibling).wait_recv()

    @pl.when(pair == 1)
    def _():
        remote(cold_in.at[0], cold_in.at[0], one_send.at[0], back_recv, sibling).wait_send()
        remote(final.at[0], final.at[0], one_send.at[1], back_recv, sibling).wait_send()

    rows = 8 * NZ * GROUPS
    returned = back_cold[...].reshape(rows, half + SIDE)
    hot_back = back_hot[...].reshape(NX * HCAP, width + SIDE)
    row = iota((rows, token_count), 0)
    within = row & 7
    group = lax.div(row, 8 * NZ)
    from_x = lax.rem(x + pair + 2 * lax.div(group, NY), NX)
    from_y = lax.rem(y + lax.rem(group, NY), NY)
    chip = (from_x * NY + from_y) * NZ + lax.rem(lax.div(row, 8), NZ)
    want = chip * CAP + (within & 3)
    first = pos[0:1, :] == want
    second = pos[1:2, :] == want
    match = first | second
    pick_low = one_hot(match & (within < CAP))
    pick_high = one_hot(match & (within >= CAP))
    hot_want = CHIPS * CAP + lax.rem(iota((NX * HCAP, token_count), 0), HCAP)
    hot_first = pos[0:1, :] == hot_want
    hot_second = pos[1:2, :] == hot_want
    pick_hot = one_hot(hot_first | hot_second)
    for low, cold_pick in ((0, pick_low), (half, pick_high)):
        part = lax.dot_general(cold_pick, returned[:, :half], ROWS, preferred_element_type=F32)
        part += lax.dot_general(pick_hot, hot_back[:, low : low + half], ROWS, preferred_element_type=F32)
        total[:, low : low + half] = part
    is_x = within < CAP
    values = []
    for a, b in ((first, hot_first), (second, hot_second)):
        value = lax.dot_general(one_hot(a & is_x), returned[:, half:], ROWS, preferred_element_type=F32)
        values.append(value + lax.dot_general(one_hot(b), hot_back[:, width:], ROWS, preferred_element_type=F32))
    total[:, width:] = jnp.where(iota((token_count, SIDE), 1) == 0, values[0], values[1])
    count = token_count // 2
    own_rows[...] = total[pl.ds(pl.multiple_of(pair * count, 16), count), :]
    other_rows[...] = total[pl.ds(pl.multiple_of((1 - pair) * count, 16), count), :].astype(BF16)


def weight_kernel(cold, d_gate, d_up, d_down, w, g_gate, g_up, g_down, h_gate, h_up, h_down):
    width = g_gate.shape[1]
    for grads, out in ((d_gate, g_gate), (d_up, g_up), (d_down, g_down)):
        out[...] = lax.dot_general(grads[...], cold[:, :width], ROWS, preferred_element_type=F32).astype(BF16)
    sums = w[0].astype(F32)
    for k in range(1, w.shape[0]):
        sums += w[k].astype(F32)
    h_gate[...] = sums[0:UNIT].astype(BF16)
    h_up[...] = sums[UNIT : 2 * UNIT].astype(BF16)
    h_down[...] = sums[2 * UNIT : 3 * UNIT].astype(BF16)


def shape(*dims, dtype=BF16):
    return jax.ShapeDtypeStruct(dims, dtype)


def local(tokens, grad_out, gate_probs, expert_ids, route_slots, hot_flags, owner_slot, cold_gate, cold_up, cold_down, hot_gate, hot_up, hot_down):
    token_count, width = tokens.shape
    wide, half = width + SIDE, width // 2
    ff = cold_gate.shape[1]
    units = 16 * RING
    dma = pltpu.SemaphoreType.DMA
    packed = half + SIDE
    lines = 8 * NZ
    hot_rows = 2 * NX * HCAP
    own_rows, other_rows, back_w, rows, d_gate, d_up, d_down = pl.pallas_call(
        layer_kernel,
        out_shape=(shape(token_count // 2, wide, dtype=F32), shape(token_count // 2, wide), shape(NZ, 16, width), shape(2 * CHIPS, 8, wide)) + (shape(16 * CHIPS, ff),) * 3,
        in_specs=[spec(pltpu.SMEM)] * 2 + [spec(VMEM)] * 8 + [spec(pl.ANY)] * 3,
        out_specs=[spec(VMEM)] * 2 + [spec(pl.ANY)] * 5,
        scratch_shapes=[
            VMEM((2, token_count), jnp.int32), VMEM((GROUPS * NZ, 8, packed), BF16), VMEM((NX, HCAP, wide), BF16), VMEM((token_count, wide), F32),
            VMEM((ff, width), BF16), VMEM((ff, width), BF16), VMEM((ff, width), BF16),
            VMEM((GROUPS * NZ, 8, wide), BF16), VMEM((HCAP, wide), BF16), VMEM((HCAP, width), BF16), VMEM((16, width), BF16),
            VMEM((2 * CHIPS, 8, wide), BF16), VMEM((hot_rows, wide), BF16), VMEM((hot_rows, width), BF16), VMEM((units, width), BF16),
            VMEM((16 * CHIPS, ff), BF16), VMEM((16 * CHIPS, ff), BF16), VMEM((16 * CHIPS, ff), BF16), VMEM((2 * hot_rows, units), BF16),
            VMEM((16 * CHIPS, packed), F32), VMEM((2 * GROUPS, lines, packed), BF16), VMEM((2 * GROUPS, lines, packed), BF16),
            VMEM((GROUPS, lines, packed), BF16), VMEM((GROUPS, lines, packed), BF16), VMEM((GROUPS * NZ, 8, packed), BF16),
            VMEM((hot_rows, wide), F32), VMEM((NX * HCAP, wide), BF16), VMEM((NX * HCAP, wide), BF16), VMEM((NX * HCAP, wide), BF16), VMEM((NZ * 16, width), F32), VMEM((NZ * 16, width), BF16), VMEM((NZ * 16, width), BF16), VMEM((NZ * 16, width), BF16),
            dma((3,)), dma, dma((GROUPS,)), dma((2,)), dma((2,)), dma, dma, dma((GROUPS,)), dma((GROUPS,)),
            dma((2 * GROUPS + 2,)), dma((2 * GROUPS + 2,)), dma((2 * GROUPS + 1,)), dma((2 * GROUPS + 1,)),
            dma((GROUPS,)), dma((GROUPS,)), dma, dma, dma, dma, dma, dma, dma((2,)), dma((2,)), dma((2,)), dma((4,)), dma((3,)),
        ],
        compiler_params=params(collective_id=0, has_side_effects=True),
    )(hot_flags, owner_slot, expert_ids.T, route_slots.T, gate_probs.T, tokens, grad_out, hot_gate, hot_up, hot_down, cold_gate[0], cold_up[0], cold_down[0])

    swapped = lax.ppermute(other_rows, "pair", [(0, 1), (1, 0)])
    count = 16 * CHIPS
    g_gate, g_up, g_down, h_gate, h_up, h_down = pl.pallas_call(
        weight_kernel,
        out_shape=(shape(ff, width),) * 3 + (shape(UNIT, width),) * 3,
        in_specs=[spec(VMEM)] * 5,
        out_specs=[spec(VMEM)] * 6,
        cost_estimate=pl.CostEstimate(flops=6 * count * ff * width, bytes_accessed=2 * count * (wide + 3 * ff) + 6 * ff * width, transcendentals=0),
        compiler_params=params(),
    )(rows.reshape(count, wide), d_gate, d_up, d_down, back_w)
    summed = own_rows + swapped.astype(F32)
    return (summed[:, :width].astype(BF16), summed[:, width : width + 2], g_gate[None], g_up[None], g_down[None], h_gate, h_up, h_down)


def solution(mesh):
    split = P(("dp", "pair"), None)
    cold = P("dp", "pair", None)
    return jax.shard_map(
        local,
        mesh=mesh,
        in_specs=(P("dp", None),) * 5 + (P(), P()) + (cold,) * 3 + (split,) * 3,
        out_specs=(split, split, cold, cold, cold, split, split, split),
        check_vma=False,
    )
```
